32 devices in a mesh: ctx: 8 (over y, x, core), tp: 4 (over z).
Axes of the slice: x: 2, y: 2, z: 4, core: 2. Of those that a mesh axis runs over, the one named last changes fastest.
Arguments:
- queries: bfloat16 [5120, 4096], P('ctx', 'tp'), may hold values from -6 to 6
- key_rows: bfloat16 [5120, 1024], P(('ctx', 'tp')), may hold values from -6 to 6
- value_rows: bfloat16 [5120, 1024], P(('ctx', 'tp')), may hold values from -6 to 6
- out_grad: bfloat16 [5120, 4096], P('ctx', 'tp'), may hold values from -6 to 6
- block_list: int32 [40, 8], P('ctx'), may hold values from 0 to 39, as said below
Outputs:
- attended: bfloat16 [5120, 4096], P('ctx', 'tp')
- query_grad: bfloat16 [5120, 4096], P('ctx', 'tp')
- key_grad: bfloat16 [5120, 1024], P(('ctx', 'tp'))
- value_grad: bfloat16 [5120, 1024], P(('ctx', 'tp'))
The draws below stay inside these ranges and needn't reach their ends.
Inputs may be any that keep to these rules, and one draw needn't show every extreme that they name: `block_list`: row i: columns 0 and 1 are two different global blocks, the same in every row; columns 2, 3, 4 are (i - 1) mod 40, i, (i + 1) mod 40; columns 5 to 7 are random blocks. Shard s holds blocks s * 5 to (s + 1) * 5 - 1. The random entries of the 5 rows of one shard name blocks of any one shard at most 2 times, and exactly 2 times for some pair of shards in every draw.
All inputs are finite; a program needn't handle non-finite values.
Results may differ from the reference program's by a relative error of at most 0.025.
Values may be sent and summed in bfloat16 or wider, within the bound.
No kernel may reach another device: no remote copies, remote signals or barrier semaphores. Data moves between devices by JAX's collectives and lax.ppermute only.
A program may use at most 192 MiB of HBM per device.

```python
import jax
import jax.numpy as jnp
from jax import lax

H = 32
KVH = 8
HD = 128
BLK = 128
RAND = 3
TOKENS = 5120
NBLK = 40
BLK_DEV = 5
LIST = 8
CAP = 2


def key_field(key):
    drawn = jax.random.normal(jax.random.fold_in(key, 101), (TOKENS, KVH * HD), jnp.float32)
    return jnp.clip(drawn, -6.0, 6.0)


def draw_key_rows(key, part):
    return key_field(key).astype(jnp.bfloat16)


def draw_queries(key, part):
    drawn = jax.random.normal(jax.random.fold_in(key, 201), (TOKENS, H * HD), jnp.float32)
    return jnp.clip(drawn, -6.0, 6.0).astype(jnp.bfloat16)


def draw_block_list(key, part):
    shard_count = NBLK // BLK_DEV
    slot_count = shard_count * CAP
    picked = RAND * BLK_DEV
    row_index = jnp.arange(NBLK, dtype=jnp.int32)
    first_global = jax.random.randint(jax.random.fold_in(key, 1), (), 0, NBLK, dtype=jnp.int32)
    second_global = (first_global + 1 + jax.random.randint(jax.random.fold_in(key, 2), (), 0, NBLK - 1, dtype=jnp.int32)) % NBLK
    heat = jax.random.randint(jax.random.fold_in(key, 3), (shard_count,), 0, 8, dtype=jnp.int32)
    heat = heat * heat
    noise = jax.random.randint(jax.random.fold_in(key, 4), (shard_count, slot_count), 0, 256, dtype=jnp.int32)
    slot_index = jnp.arange(slot_count, dtype=jnp.int32)
    ranking = (heat[slot_index // CAP][None, :] * 64 + noise) * slot_count + slot_index[None, :]
    unused, chosen = lax.top_k(ranking, picked)
    mixing = jax.random.randint(jax.random.fold_in(key, 5), (shard_count, picked), 0, 1 << 20, dtype=jnp.int32)
    mixing = mixing * picked + jnp.arange(picked, dtype=jnp.int32)[None, :]
    shuffle = jnp.argsort(mixing, axis=1, stable=True)
    chosen = jnp.take_along_axis(chosen, shuffle, axis=1).astype(jnp.int32)
    owners = chosen // CAP
    inside = jax.random.randint(jax.random.fold_in(key, 6), (shard_count, picked), 0, BLK_DEV, dtype=jnp.int32)
    random_part = (owners * BLK_DEV + inside).reshape(NBLK, RAND)
    globals_part = jnp.stack([jnp.broadcast_to(first_global, (NBLK,)), jnp.broadcast_to(second_global, (NBLK,))], axis=1)
    window_part = jnp.stack([(row_index - 1 + NBLK) % NBLK, row_index, (row_index + 1) % NBLK], axis=1)
    return jnp.concatenate([globals_part, window_part, random_part], axis=1).astype(jnp.int32)


def block_levels(rng, shape, pieces, least, top_value):
    def one(axis_at, parts):
        heights = jax.random.uniform(jax.random.fold_in(jax.random.fold_in(rng, 6), axis_at), (parts,), jnp.float32, least / len(pieces), top_value / len(pieces))
        return jnp.repeat(jnp.exp(heights), shape[axis_at] // parts).reshape((-1,) + (1,) * (len(shape) - axis_at - 1))

    level = one(*pieces[0])
    for cut in pieces[1:]:
        level = level * one(*cut)
    return level


def centred(stream_key, shape, spread, reach, shards=(), kind=jnp.bfloat16):
    gain = block_levels(stream_key, shape, shards, -0.22, 0.18) if shards else 1.0
    entries = jax.random.normal(stream_key, shape, jnp.float32) * spread * gain
    return jnp.minimum(jnp.maximum(entries, -reach), reach).astype(kind)


def setup_inputs(seed: int = 0) -> dict:
    splits = jax.random.split(jax.random.key(seed), 6)
    queries = draw_queries(jax.random.fold_in(splits[5], 71), 0)
    key_rows = draw_key_rows(jax.random.fold_in(splits[5], 71), 0)
    value_rows = centred(splits[2], (TOKENS, KVH * HD), 1.0, 6.0, ((0, 32),))
    out_grad = centred(splits[3], (TOKENS, H * HD), 1.0, 6.0, ((0, 8), (1, 4)))
    block_list = draw_block_list(jax.random.fold_in(splits[5], 71), 0)
    return {"queries": queries, "key_rows": key_rows, "value_rows": value_rows, "out_grad": out_grad, "block_list": block_list}


def reference(queries, key_rows, value_rows, out_grad, block_list):
    inverse_root = float(HD) ** -0.5
    group_size = H // KVH
    key_blocks = key_rows.reshape(NBLK, BLK, KVH, HD)
    value_blocks = value_rows.reshape(NBLK, BLK, KVH, HD)
    query_blocks = queries.reshape(NBLK, BLK, KVH, group_size, HD)
    grad_blocks = out_grad.reshape(NBLK, BLK, KVH, group_size, HD)

    def one_block(totals, inputs):
        key_acc, value_acc = totals
        query_tile, grad_tile, listed = inputs
        listed = listed.astype(jnp.int32)
        keys_here = key_blocks[listed].reshape(LIST * BLK, KVH, HD).astype(jnp.float32)
        values_here = value_blocks[listed].reshape(LIST * BLK, KVH, HD).astype(jnp.float32)
        query_f = query_tile.astype(jnp.float32)
        grad_f = grad_tile.astype(jnp.float32)
        scores = jnp.einsum("qkgd,nkd->kgqn", query_f, keys_here) * inverse_root
        row_max = jnp.max(scores, axis=-1, keepdims=True)
        logsum = row_max + jnp.log(jnp.sum(jnp.exp(scores - row_max), axis=-1, keepdims=True))
        weights_f = jnp.exp(scores - logsum)
        weights_low = lax.optimization_barrier(weights_f.astype(jnp.bfloat16)).astype(jnp.float32)
        attended = jnp.einsum("kgqn,nkd->qkgd", weights_low, values_here).astype(jnp.bfloat16)
        attended_f = lax.optimization_barrier(attended).astype(jnp.float32)
        row_delta = jnp.transpose(jnp.sum(grad_f * attended_f, axis=-1), (1, 2, 0))
        dweights = jnp.einsum("qkgd,nkd->kgqn", grad_f, values_here)
        dscores = weights_f * (dweights - row_delta[..., None])
        dscores_low = lax.optimization_barrier(dscores.astype(jnp.bfloat16)).astype(jnp.float32)
        query_grad = (jnp.einsum("kgqn,nkd->qkgd", dscores_low, keys_here) * inverse_root).astype(jnp.bfloat16)
        value_part = jnp.einsum("kgqn,qkgd->nkd", weights_low, grad_f)
        key_part = jnp.einsum("kgqn,qkgd->nkd", dscores_low, query_f) * inverse_root
        key_acc = key_acc.at[listed].add(key_part.reshape(LIST, BLK, KVH, HD))
        value_acc = value_acc.at[listed].add(value_part.reshape(LIST, BLK, KVH, HD))
        return (key_acc, value_acc), (attended, query_grad)

    empty_acc = jnp.zeros((NBLK, BLK, KVH, HD), jnp.float32)
    (key_acc, value_acc), (attended, query_grad) = lax.scan(
        one_block, (empty_acc, empty_acc), (query_blocks, grad_blocks, block_list))
    return (attended.reshape(TOKENS, H * HD),
            query_grad.reshape(TOKENS, H * HD),
            key_acc.reshape(TOKENS, KVH * HD).astype(jnp.bfloat16),
            value_acc.reshape(TOKENS, KVH * HD).astype(jnp.bfloat16))
```

```python
import functools

import jax
import jax.numpy as jnp
from jax import lax
from jax.experimental import pallas as pl
from jax.experimental.pallas import tpu as pltpu
from jax.sharding import PartitionSpec as P

HD = 128
BLK = 128
GLOB = 2
WIN = 3
RAND = 3


def padded_2(cells, sides, width):
    for axis, dim in sides:
        count = lax.axis_size(axis)
        head = lax.slice_in_dim(cells, 0, width, axis=dim)
        tail = lax.slice_in_dim(cells, cells.shape[dim] - width, cells.shape[dim], axis=dim)
        cells = jnp.concatenate(
            [
                lax.ppermute(tail, axis, [(i, (i + 1) % count) for i in range(count)]),
                cells,
                lax.ppermute(head, axis, [((i + 1) % count, i) for i in range(count)]),
            ],
            axis=dim,
        )
    return cells


def spread(x, axis, root):
    mine = lax.axis_index(axis) == root
    return lax.psum(jnp.where(mine, x, jnp.zeros_like(x)), axis)


def shifted(value, axis, steps):
    count = lax.axis_size(axis)
    pairs = [(source, (source + steps) % count) for source in range(count)]
    return lax.ppermute(value, axis, pairs)


def attend_block(tiles):
    query_tile, grad_tile, keys_tile, values_tile = tiles
    inverse_root = float(HD) ** (-0.5)
    scores = (
        jnp.einsum("qkgd,nkd->kgqn", query_tile, keys_tile, preferred_element_type=jnp.float32)
        * inverse_root
    )
    row_max = jnp.max(scores, axis=-1, keepdims=True)
    logsum = row_max + jnp.log(jnp.sum(jnp.exp(scores - row_max), axis=-1, keepdims=True))
    weights_f = jnp.exp(scores - logsum)
    weights_low = weights_f.astype(jnp.bfloat16)
    attended = jnp.einsum(
        "kgqn,nkd->qkgd", weights_low, values_tile, preferred_element_type=jnp.float32
    ).astype(jnp.bfloat16)
    row_delta = jnp.sum(grad_tile.astype(jnp.float32) * attended.astype(jnp.float32), axis=-1)
    row_delta = jnp.transpose(row_delta, (1, 2, 0))
    dweights = jnp.einsum(
        "qkgd,nkd->kgqn", grad_tile, values_tile, preferred_element_type=jnp.float32
    )
    dscores_low = (weights_f * (dweights - row_delta[..., None])).astype(jnp.bfloat16)
    query_grad = (
        jnp.einsum("kgqn,nkd->qkgd", dscores_low, keys_tile, preferred_element_type=jnp.float32)
        * inverse_root
    ).astype(jnp.bfloat16)
    value_part = jnp.einsum(
        "kgqn,qkgd->nkd", weights_low, grad_tile, preferred_element_type=jnp.float32
    )
    key_part = (
        jnp.einsum("kgqn,qkgd->nkd", dscores_low, query_tile, preferred_element_type=jnp.float32)
        * inverse_root
    )
    return (attended, query_grad, key_part, value_part)


def sparse_plan(queries, key_rows, value_rows, out_grad, block_list):
    tokens_here = queries.shape[0]
    block_count = tokens_here // BLK
    shard_total = lax.axis_size("ctx")
    my_index = lax.axis_index("ctx")
    local_keys, local_values = (
        lax.all_to_all(key_rows, "tp", split_axis=1, concat_axis=0, tiled=True),
        lax.all_to_all(value_rows, "tp", split_axis=1, concat_axis=0, tiled=True),
    )
    head_width = local_keys.shape[1]
    kv_heads = head_width // HD
    both_width = 2 * head_width
    joined = jnp.concatenate([local_keys, local_values], axis=1)
    joined_blocks = joined.reshape(block_count, BLK, both_width)
    padded = padded_2(joined, (("ctx", 0),), BLK)
    padded = padded.reshape(block_count + 2, BLK, both_width)
    window_kv = jnp.stack(
        [padded[0:block_count], padded[1 : block_count + 1], padded[2 : block_count + 2]], axis=1
    )
    global_ids = block_list[0, 0:GLOB]
    global_owner = global_ids // block_count
    global_local = global_ids % block_count
    fetched_list = []
    for column in range(GLOB):
        owned = lax.dynamic_index_in_dim(joined_blocks, global_local[column], 0, keepdims=False)
        fetched_list.append(spread(owned, "ctx", global_owner[column]))
    global_kv = jnp.stack(fetched_list, axis=0)
    random_ids = block_list[:, GLOB + WIN :].reshape(-1)
    ref_count = random_ids.shape[0]
    capacity = (ref_count + shard_total - 1) // shard_total
    slot_count = shard_total * capacity
    ref_owner = random_ids // block_count
    ref_local = random_ids % block_count
    ref_order = jnp.arange(ref_count, dtype=jnp.int32)
    earlier = (ref_owner[:, None] == ref_owner[None, :]) & (ref_order[None, :] < ref_order[:, None])
    ref_rank = jnp.sum(earlier, axis=1)
    ref_slot = ref_owner * capacity + ref_rank
    slot_hit = ref_slot[:, None] == jnp.arange(slot_count, dtype=jnp.int32)[None, :]
    wanted = jnp.sum(jnp.where(slot_hit, ref_local[:, None] + 1, 0), axis=0) - 1
    asked = lax.all_to_all(
        wanted.reshape(shard_total, capacity), "ctx", split_axis=0, concat_axis=0, tiled=True
    )
    valid_ask = asked >= 0
    served = jnp.where(
        valid_ask[:, :, None, None],
        joined_blocks[jnp.maximum(asked, 0)],
        jnp.zeros((), jnp.bfloat16),
    )
    arrived = lax.all_to_all(served, "ctx", split_axis=0, concat_axis=0, tiled=True).reshape(
        slot_count, BLK, both_width
    )
    random_kv = arrived[ref_slot].reshape(block_count, RAND, BLK, both_width)
    list_len = GLOB + WIN + RAND
    global_rep = jnp.broadcast_to(global_kv[None], (block_count, GLOB, BLK, both_width))
    listed_kv = jnp.concatenate([global_rep, window_kv, random_kv], axis=1)
    keys_here = listed_kv[..., :head_width].reshape(block_count, list_len * BLK, kv_heads, HD)
    values_here = listed_kv[..., head_width:].reshape(block_count, list_len * BLK, kv_heads, HD)
    group_size = queries.shape[1] // head_width
    query_tiles = queries.reshape(block_count, BLK, kv_heads, group_size, HD)
    grad_tiles = out_grad.reshape(block_count, BLK, kv_heads, group_size, HD)
    attended, query_grad, key_part, value_part = lax.map(
        attend_block, (query_tiles, grad_tiles, keys_here, values_here)
    )
    grad_kv = jnp.concatenate(
        [
            key_part.reshape(block_count, list_len, BLK, head_width),
            value_part.reshape(block_count, list_len, BLK, head_width),
        ],
        axis=-1,
    )
    window_grad = grad_kv[:, GLOB : GLOB + WIN]
    zero_block = jnp.zeros((1, BLK, both_width), jnp.float32)
    rim_acc = (
        jnp.concatenate([window_grad[:, 0], zero_block, zero_block], axis=0)
        + jnp.concatenate([zero_block, window_grad[:, 1], zero_block], axis=0)
        + jnp.concatenate([zero_block, zero_block, window_grad[:, 2]], axis=0)
    )
    from_left = shifted(rim_acc[block_count + 1].astype(jnp.bfloat16), "ctx", 1).astype(jnp.float32)
    from_right = shifted(rim_acc[0].astype(jnp.bfloat16), "ctx", -1).astype(jnp.float32)
    own_grads = rim_acc[1 : block_count + 1]
    own_grads = own_grads.at[0].add(from_left)
    own_grads = own_grads.at[block_count - 1].add(from_right)
    global_terms = lax.psum(jnp.sum(grad_kv[:, 0:GLOB], axis=0), "ctx")
    global_place = (global_local[:, None] == jnp.arange(block_count, dtype=jnp.int32)[None, :]) & (
        global_owner == my_index
    )[:, None]
    own_grads = own_grads + jnp.einsum(
        "ro,rhn->ohn",
        global_place.astype(jnp.float32),
        global_terms,
        precision=lax.Precision.HIGHEST,
    )
    random_grad = grad_kv[:, GLOB + WIN :].reshape(ref_count, BLK, both_width)
    outgoing = jnp.zeros((slot_count, BLK, both_width), jnp.float32).at[ref_slot].set(random_grad)
    returned = lax.all_to_all(
        outgoing.reshape(shard_total, capacity, BLK, both_width).astype(jnp.bfloat16),
        "ctx",
        split_axis=0,
        concat_axis=0,
        tiled=True,
    ).astype(jnp.float32)
    returned = returned.reshape(slot_count, BLK, both_width)
    slot_place = (
        asked.reshape(slot_count)[:, None] == jnp.arange(block_count, dtype=jnp.int32)[None, :]
    ).astype(jnp.float32)
    own_grads = own_grads + jnp.einsum(
        "sj,sxc->jxc", slot_place, returned, precision=lax.Precision.HIGHEST
    )
    own_grads = own_grads.reshape(tokens_here, both_width).astype(jnp.bfloat16)
    key_grad, value_grad = (
        lax.all_to_all(own_grads[:, :head_width], "tp", split_axis=0, concat_axis=1, tiled=True),
        lax.all_to_all(own_grads[:, head_width:], "tp", split_axis=0, concat_axis=1, tiled=True),
    )
    return (
        attended.reshape(tokens_here, -1),
        query_grad.reshape(tokens_here, -1),
        key_grad,
        value_grad,
    )


LOG2E = 1.4426950408889634
DENSE_SHARDS = 8
NT = (((1,), (1,)), ((), ()))
TN = (((0,), (0,)), ((), ()))


def swap(value, axis, mask):
    count = lax.axis_size(axis)
    return lax.ppermute(value, axis, [(i, i ^ mask) for i in range(count)])


def rows_of(quarter, shard, spot, tokens, me_tp):
    return pl.multiple_of(shard * tokens + (spot ^ me_tp) * quarter, 16)


def gather_pieces(piece_refs, pieces, tokens, me_tp, buffer, sems):
    copies = []
    for ref, (shard, first, count) in zip(piece_refs, pieces):
        quarter = ref.shape[1]
        for at in range(count):
            start = rows_of(quarter, shard, first + at, tokens, me_tp)
            copies.append(
                pltpu.make_async_copy(
                    ref.at[at], buffer.at[pl.ds(start, quarter)], sems.at[len(copies)]
                )
            )
    for copy in copies:
        copy.start()
    for copy in copies:
        copy.wait()


def scatter_pieces(acc, buffer, targets, tokens, me_tp, sems):
    copies = []
    for ref, shard in targets:
        spots, quarter = ref.shape[0], ref.shape[1]
        rows = slice(shard * tokens, (shard + 1) * tokens)
        buffer[rows] = acc[rows].astype(buffer.dtype)
        for spot in range(spots):
            start = rows_of(quarter, shard, spot, tokens, me_tp)
            copy = pltpu.make_async_copy(
                buffer.at[pl.ds(start, quarter)], ref.at[spot], sems.at[len(copies)]
            )
            copy.start()
            copies.append(copy)
    for copy in copies:
        copy.wait()


def list_rows(place_ref, row, width, buffer, listed):
    places = []
    for column in range(width):
        place = pl.multiple_of(place_ref[row * width + column] * BLK, BLK)
        listed[0, column * BLK : (column + 1) * BLK] = buffer[pl.ds(place, BLK)]
        places.append(place)
    return places


def fold(value, op):
    rows, width = value.shape
    return op(value.reshape(rows // 8, 8, width), axis=0)


def probs_kernel(pieces, tokens, width, heads, group, place_ref, tp_ref, *refs):
    count = len(pieces)
    query_ref, grad_ref = refs[0:2]
    piece_refs = refs[2 : 2 + count]
    exp_ref, query_t_ref, grad_t_ref, inv_ref, listed_ref = refs[2 + count : 7 + count]
    out_refs = refs[7 + count : 11 + count]
    buffer, acc, score_ref, load_sems, store_sems = refs[11 + count :]
    row = pl.program_id(0)
    me_tp = tp_ref[0]

    @pl.when(row == 0)
    def _():
        acc[...] = jnp.zeros_like(acc)
        gather_pieces(piece_refs, pieces, tokens, me_tp, buffer, load_sems)

    places = list_rows(place_ref, row, width, buffer, listed_ref)
    factor = LOG2E * float(HD) ** (-0.5)
    for head in range(heads):
        lanes = slice(head * HD, (head + 1) * HD)
        parts = [
            slice((head * group + g) * HD, (head * group + g + 1) * HD) for g in range(group)
        ]
        query_t = jnp.concatenate([query_ref[:, part].T for part in parts], axis=1)
        grad_t = jnp.concatenate([grad_ref[:, part].T for part in parts], axis=1)
        query_t_ref[0, head] = query_t
        score_ref[head] = jnp.dot(
            listed_ref[0, :, lanes], query_t, preferred_element_type=jnp.float32
        )
        top = None
        for column in range(width):
            chunk = slice(column * BLK, (column + 1) * BLK)
            here = fold(score_ref[head, chunk], jnp.max)
            top = here if top is None else jnp.maximum(top, here)
        top = jnp.max(top, axis=0, keepdims=True) * factor
        total = None
        for column in range(width):
            chunk = slice(column * BLK, (column + 1) * BLK)
            weight = jnp.exp2(score_ref[head, chunk] * factor - top)
            exp_ref[0, head, chunk] = weight.astype(jnp.bfloat16)
            here = fold(weight, jnp.sum)
            total = here if total is None else total + here
        inverse = 1.0 / jnp.sum(total, axis=0, keepdims=True)
        inv_ref[0, head] = jnp.broadcast_to(inverse, inv_ref.shape[2:])
        grad_low = (grad_t.astype(jnp.float32) * inverse).astype(jnp.bfloat16)
        grad_t_ref[0, head] = grad_low
        part = lax.dot_general(exp_ref[0, head], grad_low, NT, preferred_element_type=jnp.float32)
        for column in range(width):
            acc[pl.ds(places[column], BLK), lanes] += part[column * BLK : (column + 1) * BLK]

    @pl.when(row == pl.num_programs(0) - 1)
    def _():
        write_out(acc, buffer, out_refs, tokens, me_tp, store_sems)


def write_out(acc, buffer, out_refs, tokens, me_tp, sems):
    near_ref, far3_ref, far12_ref, far0_ref = out_refs
    targets = [(far3_ref, 7), (far12_ref.at[0], 3), (far12_ref.at[1], 5), (far0_ref, 1)]
    targets += [(near_ref.at[k], 2 * k) for k in (3, 1, 2, 0)]
    scatter_pieces(acc, buffer, targets, tokens, me_tp, sems)


def scores_kernel(pieces, tokens, width, heads, place_ref, tp_ref, *refs):
    count = len(pieces)
    exp_ref, query_t_ref, grad_t_ref, inv_ref = refs[0:4]
    piece_refs = refs[4 : 4 + count]
    ds_ref, listed_ref = refs[4 + count : 6 + count]
    out_refs = refs[6 + count : 10 + count]
    buffer, acc, dprob_ref, load_sems, store_sems = refs[10 + count :]
    row = pl.program_id(0)
    me_tp = tp_ref[0]

    @pl.when(row == 0)
    def _():
        acc[...] = jnp.zeros_like(acc)
        gather_pieces(piece_refs, pieces, tokens, me_tp, buffer, load_sems)

    places = list_rows(place_ref, row, width, buffer, listed_ref)
    for head in range(heads):
        lanes = slice(head * HD, (head + 1) * HD)
        dprob_ref[head] = jnp.dot(
            listed_ref[0, :, lanes], grad_t_ref[0, head], preferred_element_type=jnp.float32
        )
        delta = None
        for column in range(width):
            chunk = slice(column * BLK, (column + 1) * BLK)
            weight = exp_ref[0, head, chunk].astype(jnp.float32)
            here = fold(weight * dprob_ref[head, chunk], jnp.sum)
            delta = here if delta is None else delta + here
        delta = jnp.sum(delta, axis=0, keepdims=True) * inv_ref[0, head, 0:1]
        for column in range(width):
            chunk = slice(column * BLK, (column + 1) * BLK)
            weight = exp_ref[0, head, chunk].astype(jnp.float32)
            ds_ref[0, head, chunk] = (weight * (dprob_ref[head, chunk] - delta)).astype(
                jnp.bfloat16
            )
        part = lax.dot_general(
            ds_ref[0, head], query_t_ref[0, head], NT, preferred_element_type=jnp.float32
        ) * float(HD) ** (-0.5)
        for column in range(width):
            acc[pl.ds(places[column], BLK), lanes] += part[column * BLK : (column + 1) * BLK]

    @pl.when(row == pl.num_programs(0) - 1)
    def _():
        write_out(acc, buffer, out_refs, tokens, me_tp, store_sems)


def rows_kernel(heads, group, exp_ref, ds_ref, inv_ref, keys_ref, values_ref, out_ref, dq_ref):
    for head in range(heads):
        lanes = slice(head * HD, (head + 1) * HD)
        attended = lax.dot_general(
            values_ref[0, :, lanes], exp_ref[0, head], TN, preferred_element_type=jnp.float32
        )
        attended = attended * inv_ref[0, head, 0:1]
        query_grad = lax.dot_general(
            keys_ref[0, :, lanes], ds_ref[0, head], TN, preferred_element_type=jnp.float32
        ) * float(HD) ** (-0.5)
        for g in range(group):
            part = slice((head * group + g) * HD, (head * group + g + 1) * HD)
            out_ref[:, part] = attended[:, g * BLK : (g + 1) * BLK].T.astype(jnp.bfloat16)
            dq_ref[:, part] = query_grad[:, g * BLK : (g + 1) * BLK].T.astype(jnp.bfloat16)


def to_head_groups(rows):
    me = lax.axis_index("tp")
    count = lax.axis_size("tp")
    width = rows.shape[1] // count
    parts = []
    for mask in range(count):
        part = lax.dynamic_slice_in_dim(rows, (me ^ mask) * width, width, 1)
        parts.append(part if mask == 0 else swap(part, "tp", mask))
    return jnp.stack(parts)


def to_quarters(pieces):
    me = lax.axis_index("tp")
    count, quarter, width = pieces.shape
    out = jnp.zeros((quarter, count * width), pieces.dtype)
    for mask in range(count):
        part = pieces[mask] if mask == 0 else swap(pieces[mask], "tp", mask)
        out = lax.dynamic_update_slice(out, part, (0, (me ^ mask) * width))
    return out


def gather_shards(own):
    half = own.shape[0] // 2
    across = swap(own, "ctx", 2)
    along = swap(own, "ctx", 4)
    first = swap(along[:half], "ctx", 2)
    second = swap(across[half:], "ctx", 4)
    near = [own, across, along, first, second]
    far = [swap(part, "ctx", 1) for part in near]
    return near + far


def shard_pieces(count):
    half = count // 2
    near = [(0, 0, count), (2, 0, count), (4, 0, count), (6, 0, half), (6, half, half)]
    return near + [(shard + 1, first, many) for shard, first, many in near]


def sum_shards(near, far3, far12, far0):
    half = near.shape[1] // 2
    got3 = swap(far3, "ctx", 1)
    got12 = swap(far12, "ctx", 1)
    got0 = swap(far0, "ctx", 1)
    diag_a = near[3, :half] + got3[:half]
    diag_b = near[3, half:] + got3[half:]
    from_x = swap(diag_a, "ctx", 2)
    from_y = swap(diag_b, "ctx", 4)
    across_a = near[1, :half] + got12[0, :half]
    along_b = near[2, half:] + got12[1, half:]
    own_a = swap(across_a, "ctx", 2)
    own_b = swap(along_b, "ctx", 4)
    across_b = near[1, half:] + got12[0, half:] + from_y
    along_a = near[2, :half] + got12[1, :half] + from_x
    more_b = swap(across_b, "ctx", 2)
    more_a = swap(along_a, "ctx", 4)
    own = near[0] + got0
    return own + jnp.concatenate([own_a + more_a, own_b + more_b], axis=0)


def dense_plan(queries, key_rows, value_rows, out_grad, block_list):
    tokens = queries.shape[0]
    blocks = tokens // BLK
    shard_total = lax.axis_size("ctx")
    quarters = lax.axis_size("tp")
    width = block_list.shape[1]
    head_width = key_rows.shape[1] // quarters
    heads = head_width // HD
    group = queries.shape[1] // head_width
    rows = shard_total * tokens
    me_ctx = lax.axis_index("ctx")
    me_tp = lax.axis_index("tp").reshape(1)
    places = ((block_list // blocks) ^ me_ctx) * blocks + block_list % blocks
    places = places.reshape(-1)
    quarter = tokens // quarters
    pieces = shard_pieces(quarters)
    list_len = width * BLK
    query_rows = group * BLK
    far_pieces = shard_total * quarters

    any_spec = pl.BlockSpec(memory_space=pl.ANY)

    def per_row(*shape):
        return pl.BlockSpec((1, *shape), lambda i, *_: (i,) + (0,) * len(shape))

    def flat(columns):
        return pl.BlockSpec((BLK, columns), lambda i, *_: (i, 0))

    def stash(*shape, dtype=jnp.bfloat16):
        return jax.ShapeDtypeStruct((blocks, *shape), dtype)

    sum_shapes = [
        jax.ShapeDtypeStruct((shard_total // 2, quarters, quarter, head_width), jnp.bfloat16),
        jax.ShapeDtypeStruct((quarters, quarter, head_width), jnp.bfloat16),
        jax.ShapeDtypeStruct((2, quarters, quarter, head_width), jnp.bfloat16),
        jax.ShapeDtypeStruct((quarters, quarter, head_width), jnp.bfloat16),
    ]
    scratch = [
        pltpu.VMEM((rows, head_width), jnp.bfloat16),
        pltpu.VMEM((rows, head_width), jnp.float32),
        pltpu.VMEM((heads, list_len, query_rows), jnp.float32),
        pltpu.SemaphoreType.DMA((far_pieces,)),
        pltpu.SemaphoreType.DMA((far_pieces,)),
    ]
    params = pltpu.CompilerParams(vmem_limit_bytes=48 * 2**20)
    flops = 4 * blocks * heads * list_len * query_rows * HD
    big = (heads, list_len, query_rows)
    small = (heads, HD, query_rows)
    lse = (heads, 8, query_rows)
    listed = (list_len, head_width)

    keys = gather_shards(to_head_groups(key_rows))
    values = gather_shards(to_head_groups(value_rows))

    made = pl.pallas_call(
        functools.partial(probs_kernel, pieces, tokens, width, heads, group),
        grid_spec=pltpu.PrefetchScalarGridSpec(
            num_scalar_prefetch=2,
            grid=(blocks,),
            in_specs=[flat(queries.shape[1]), flat(queries.shape[1])] + [any_spec] * len(pieces),
            out_specs=[per_row(*big), per_row(*small), per_row(*small), per_row(*lse), per_row(*listed)]
            + [any_spec] * 4,
            scratch_shapes=scratch,
        ),
        out_shape=[
            stash(*big),
            stash(*small),
            stash(*small),
            stash(*lse, dtype=jnp.float32),
            stash(*listed),
        ]
        + sum_shapes,
        compiler_params=params,
        cost_estimate=pl.CostEstimate(flops=flops, bytes_accessed=2**24, transcendentals=0),
        name="probs",
    )(places, me_tp, queries, out_grad, *keys)
    exp_low, query_t, grad_t, inverse, keys_listed = made[:5]
    value_sum = sum_shards(*made[5:])

    made = pl.pallas_call(
        functools.partial(scores_kernel, pieces, tokens, width, heads),
        grid_spec=pltpu.PrefetchScalarGridSpec(
            num_scalar_prefetch=2,
            grid=(blocks,),
            in_specs=[per_row(*big), per_row(*small), per_row(*small), per_row(*lse)]
            + [any_spec] * len(pieces),
            out_specs=[per_row(*big), per_row(*listed)] + [any_spec] * 4,
            scratch_shapes=scratch,
        ),
        out_shape=[stash(*big), stash(*listed)] + sum_shapes,
        compiler_params=params,
        cost_estimate=pl.CostEstimate(flops=flops, bytes_accessed=2**24, transcendentals=0),
        name="scores",
    )(places, me_tp, exp_low, query_t, grad_t, inverse, *values)
    ds_low, values_listed = made[:2]
    key_sum = sum_shards(*made[2:])

    attended, query_grad = pl.pallas_call(
        functools.partial(rows_kernel, heads, group),
        grid=(blocks,),
        in_specs=[per_row(*big), per_row(*big), per_row(*lse), per_row(*listed), per_row(*listed)],
        out_specs=[flat(queries.shape[1])] * 2,
        out_shape=[jax.ShapeDtypeStruct(queries.shape, jnp.bfloat16)] * 2,
        compiler_params=params,
        cost_estimate=pl.CostEstimate(flops=flops, bytes_accessed=2**24, transcendentals=0),
        name="rows",
    )(exp_low, ds_low, inverse, keys_listed, values_listed)
    return attended, query_grad, to_quarters(key_sum), to_quarters(value_sum)


def solution(mesh):
    dense = mesh.shape["ctx"] == DENSE_SHARDS and mesh.shape["tp"] % 4 == 0
    in_specs = (
        P("ctx", "tp"),
        P(("ctx", "tp"), None),
        P(("ctx", "tp"), None),
        P("ctx", "tp"),
        P("ctx", None),
    )
    out_specs = (P("ctx", "tp"), P("ctx", "tp"), P(("ctx", "tp"), None), P(("ctx", "tp"), None))
    return jax.shard_map(
        dense_plan if dense else sparse_plan,
        mesh=mesh,
        in_specs=in_specs,
        out_specs=out_specs,
        check_vma=False,
    )
```

```python
import functools

import jax
import jax.numpy as jnp
from jax import lax
from jax.experimental import pallas as pl
from jax.experimental.pallas import tpu as pltpu
from jax.sharding import PartitionSpec as P

HD = 128
BLK = 128
GLOB = 2
WIN = 3
RAND = 3


def padded_2(cells, sides, width):
    for axis, dim in sides:
        count = lax.axis_size(axis)
        head = lax.slice_in_dim(cells, 0, width, axis=dim)
        tail = lax.slice_in_dim(cells, cells.shape[dim] - width, cells.shape[dim], axis=dim)
        cells = jnp.concatenate(
            [
                lax.ppermute(tail, axis, [(i, (i + 1) % count) for i in range(count)]),
                cells,
                lax.ppermute(head, axis, [((i + 1) % count, i) for i in range(count)]),
            ],
            axis=dim,
        )
    return cells


def spread(x, axis, root):
    mine = lax.axis_index(axis) == root
    return lax.psum(jnp.where(mine, x, jnp.zeros_like(x)), axis)


def shifted(value, axis, steps):
    count = lax.axis_size(axis)
    pairs = [(source, (source + steps) % count) for source in range(count)]
    return lax.ppermute(value, axis, pairs)


def attend_block(tiles):
    query_tile, grad_tile, keys_tile, values_tile = tiles
    inverse_root = float(HD) ** (-0.5)
    scores = (
        jnp.einsum("qkgd,nkd->kgqn", query_tile, keys_tile, preferred_element_type=jnp.float32)
        * inverse_root
    )
    row_max = jnp.max(scores, axis=-1, keepdims=True)
    logsum = row_max + jnp.log(jnp.sum(jnp.exp(scores - row_max), axis=-1, keepdims=True))
    weights_f = jnp.exp(scores - logsum)
    weights_low = weights_f.astype(jnp.bfloat16)
    attended = jnp.einsum(
        "kgqn,nkd->qkgd", weights_low, values_tile, preferred_element_type=jnp.float32
    ).astype(jnp.bfloat16)
    row_delta = jnp.sum(grad_tile.astype(jnp.float32) * attended.astype(jnp.float32), axis=-1)
    row_delta = jnp.transpose(row_delta, (1, 2, 0))
    dweights = jnp.einsum(
        "qkgd,nkd->kgqn", grad_tile, values_tile, preferred_element_type=jnp.float32
    )
    dscores_low = (weights_f * (dweights - row_delta[..., None])).astype(jnp.bfloat16)
    query_grad = (
        jnp.einsum("kgqn,nkd->qkgd", dscores_low, keys_tile, preferred_element_type=jnp.float32)
        * inverse_root
    ).astype(jnp.bfloat16)
    value_part = jnp.einsum(
        "kgqn,qkgd->nkd", weights_low, grad_tile, preferred_element_type=jnp.float32
    )
    key_part = (
        jnp.einsum("kgqn,qkgd->nkd", dscores_low, query_tile, preferred_element_type=jnp.float32)
        * inverse_root
    )
    return (attended, query_grad, key_part, value_part)


def sparse_plan(queries, key_rows, value_rows, out_grad, block_list):
    tokens_here = queries.shape[0]
    block_count = tokens_here // BLK
    shard_total = lax.axis_size("ctx")
    my_index = lax.axis_index("ctx")
    local_keys, local_values = (
        lax.all_to_all(key_rows, "tp", split_axis=1, concat_axis=0, tiled=True),
        lax.all_to_all(value_rows, "tp", split_axis=1, concat_axis=0, tiled=True),
    )
    head_width = local_keys.shape[1]
    kv_heads = head_width // HD
    both_width = 2 * head_width
    joined = jnp.concatenate([local_keys, local_values], axis=1)
    joined_blocks = joined.reshape(block_count, BLK, both_width)
    padded = padded_2(joined, (("ctx", 0),), BLK)
    padded = padded.reshape(block_count + 2, BLK, both_width)
    window_kv = jnp.stack(
        [padded[0:block_count], padded[1 : block_count + 1], padded[2 : block_count + 2]], axis=1
    )
    global_ids = block_list[0, 0:GLOB]
    global_owner = global_ids // block_count
    global_local = global_ids % block_count
    fetched_list = []
    for column in range(GLOB):
        owned = lax.dynamic_index_in_dim(joined_blocks, global_local[column], 0, keepdims=False)
        fetched_list.append(spread(owned, "ctx", global_owner[column]))
    global_kv = jnp.stack(fetched_list, axis=0)
    random_ids = block_list[:, GLOB + WIN :].reshape(-1)
    ref_count = random_ids.shape[0]
    capacity = (ref_count + shard_total - 1) // shard_total
    slot_count = shard_total * capacity
    ref_owner = random_ids // block_count
    ref_local = random_ids % block_count
    ref_order = jnp.arange(ref_count, dtype=jnp.int32)
    earlier = (ref_owner[:, None] == ref_owner[None, :]) & (ref_order[None, :] < ref_order[:, None])
    ref_rank = jnp.sum(earlier, axis=1)
    ref_slot = ref_owner * capacity + ref_rank
    slot_hit = ref_slot[:, None] == jnp.arange(slot_count, dtype=jnp.int32)[None, :]
    wanted = jnp.sum(jnp.where(slot_hit, ref_local[:, None] + 1, 0), axis=0) - 1
    asked = lax.all_to_all(
        wanted.reshape(shard_total, capacity), "ctx", split_axis=0, concat_axis=0, tiled=True
    )
    valid_ask = asked >= 0
    served = jnp.where(
        valid_ask[:, :, None, None],
        joined_blocks[jnp.maximum(asked, 0)],
        jnp.zeros((), jnp.bfloat16),
    )
    arrived = lax.all_to_all(served, "ctx", split_axis=0, concat_axis=0, tiled=True).reshape(
        slot_count, BLK, both_width
    )
    random_kv = arrived[ref_slot].reshape(block_count, RAND, BLK, both_width)
    list_len = GLOB + WIN + RAND
    global_rep = jnp.broadcast_to(global_kv[None], (block_count, GLOB, BLK, both_width))
    listed_kv = jnp.concatenate([global_rep, window_kv, random_kv], axis=1)
    keys_here = listed_kv[..., :head_width].reshape(block_count, list_len * BLK, kv_heads, HD)
    values_here = listed_kv[..., head_width:].reshape(block_count, list_len * BLK, kv_heads, HD)
    group_size = queries.shape[1] // head_width
    query_tiles = queries.reshape(block_count, BLK, kv_heads, group_size, HD)
    grad_tiles = out_grad.reshape(block_count, BLK, kv_heads, group_size, HD)
    attended, query_grad, key_part, value_part = lax.map(
        attend_block, (query_tiles, grad_tiles, keys_here, values_here)
    )
    grad_kv = jnp.concatenate(
        [
            key_part.reshape(block_count, list_len, BLK, head_width),
            value_part.reshape(block_count, list_len, BLK, head_width),
        ],
        axis=-1,
    )
    window_grad = grad_kv[:, GLOB : GLOB + WIN]
    zero_block = jnp.zeros((1, BLK, both_width), jnp.float32)
    rim_acc = (
        jnp.concatenate([window_grad[:, 0], zero_block, zero_block], axis=0)
        + jnp.concatenate([zero_block, window_grad[:, 1], zero_block], axis=0)
        + jnp.concatenate([zero_block, zero_block, window_grad[:, 2]], axis=0)
    )
    from_left = shifted(rim_acc[block_count + 1].astype(jnp.bfloat16), "ctx", 1).astype(jnp.float32)
    from_right = shifted(rim_acc[0].astype(jnp.bfloat16), "ctx", -1).astype(jnp.float32)
    own_grads = rim_acc[1 : block_count + 1]
    own_grads = own_grads.at[0].add(from_left)
    own_grads = own_grads.at[block_count - 1].add(from_right)
    global_terms = lax.psum(jnp.sum(grad_kv[:, 0:GLOB], axis=0), "ctx")
    global_place = (global_local[:, None] == jnp.arange(block_count, dtype=jnp.int32)[None, :]) & (
        global_owner == my_index
    )[:, None]
    own_grads = own_grads + jnp.einsum(
        "ro,rhn->ohn",
        global_place.astype(jnp.float32),
        global_terms,
        precision=lax.Precision.HIGHEST,
    )
    random_grad = grad_kv[:, GLOB + WIN :].reshape(ref_count, BLK, both_width)
    outgoing = jnp.zeros((slot_count, BLK, both_width), jnp.float32).at[ref_slot].set(random_grad)
    returned = lax.all_to_all(
        outgoing.reshape(shard_total, capacity, BLK, both_width).astype(jnp.bfloat16),
        "ctx",
        split_axis=0,
        concat_axis=0,
        tiled=True,
    ).astype(jnp.float32)
    returned = returned.reshape(slot_count, BLK, both_width)
    slot_place = (
        asked.reshape(slot_count)[:, None] == jnp.arange(block_count, dtype=jnp.int32)[None, :]
    ).astype(jnp.float32)
    own_grads = own_grads + jnp.einsum(
        "sj,sxc->jxc", slot_place, returned, precision=lax.Precision.HIGHEST
    )
    own_grads = own_grads.reshape(tokens_here, both_width).astype(jnp.bfloat16)
    key_grad, value_grad = (
        lax.all_to_all(own_grads[:, :head_width], "tp", split_axis=0, concat_axis=1, tiled=True),
        lax.all_to_all(own_grads[:, head_width:], "tp", split_axis=0, concat_axis=1, tiled=True),
    )
    return (
        attended.reshape(tokens_here, -1),
        query_grad.reshape(tokens_here, -1),
        key_grad,
        value_grad,
    )


LOG2E = 1.4426950408889634
DENSE_SHARDS = 8
NT = (((1,), (1,)), ((), ()))
TN = (((0,), (0,)), ((), ()))


def swap(value, axis, mask):
    count = lax.axis_size(axis)
    return lax.ppermute(value, axis, [(i, i ^ mask) for i in range(count)])


def rows_of(quarter, shard, spot, tokens, me_tp):
    return pl.ds(pl.multiple_of(shard * tokens + (spot ^ me_tp) * quarter, 16), quarter)


def place_pieces(piece_refs, pieces, tokens, me_tp, buffer):
    for ref, (shard, first, count) in zip(piece_refs, pieces):
        for at in range(count):
            buffer[rows_of(ref.shape[1], shard, first + at, tokens, me_tp)] = ref[at]


def write_sums(acc, out_refs, tokens, me_tp, scale):
    near_ref, far3_ref, far12_ref, far0_ref = out_refs
    targets = [(far3_ref, 7), (far12_ref.at[0], 3), (far12_ref.at[1], 5), (far0_ref, 1)]
    targets += [(near_ref.at[k], 2 * k) for k in (3, 1, 2, 0)]
    for ref, shard in targets:
        for spot in range(ref.shape[0]):
            part = acc[rows_of(ref.shape[1], shard, spot, tokens, me_tp)]
            if scale is not None:
                part = part * scale
            ref[spot] = part.astype(ref.dtype)


def block_of(place_ref, entry):
    return pl.ds(pl.multiple_of(place_ref[entry] * BLK, BLK), BLK)


def fold(value, op):
    rows, width = value.shape
    return op(value.reshape(rows // 8, 8, width), axis=0)


def joined(op, total, value):
    return value if total is None else op(total, value)


class Units:
    def __init__(self, blocks, width, heads, group):
        self.blocks, self.width, self.heads, self.group = blocks, width, heads, group
        self.count = blocks * heads

    def rows(self, unit):
        row = unit // self.heads
        return slice(row * BLK, (row + 1) * BLK)

    def lanes(self, unit):
        head = unit % self.heads
        return slice(head * HD, (head + 1) * HD)

    def parts(self, unit):
        first = (unit % self.heads) * self.group
        return [slice((first + g) * HD, (first + g + 1) * HD) for g in range(self.group)]

    def chunks(self):
        return [(c, slice(c * BLK, (c + 1) * BLK)) for c in range(self.width)]

    def entry(self, unit, column):
        return (unit // self.heads) * self.width + column

    def stacked(self, ref, unit):
        return jnp.concatenate([ref[self.rows(unit), part] for part in self.parts(unit)], axis=0)

    def flipped(self, ref, unit):
        return jnp.concatenate([ref[self.rows(unit), part].T for part in self.parts(unit)], axis=1)


def probs_kernel(pieces, units, tokens, place_ref, tp_ref, query_ref, grad_ref, *refs):
    count = len(pieces)
    piece_refs = refs[:count]
    exp_ref, grad_t_ref, inv_ref, buffer = refs[count : count + 4]
    out_refs = refs[count + 4 : count + 8]
    acc, score_ref = refs[count + 8 :]
    me_tp = tp_ref[0]
    acc[...] = jnp.zeros_like(acc)
    place_pieces(piece_refs, pieces, tokens, me_tp, buffer)
    factor = LOG2E * float(HD) ** (-0.5)
    tops, totals = {}, {}
    for step in range(units.count + 2):
        first, second, third = step, step - 1, step - 2
        top_new = total_new = None
        if first < units.count:
            query = units.stacked(query_ref, first)
        if 0 <= second < units.count:
            top = jnp.max(tops[second], axis=0, keepdims=True) * factor
        if 0 <= third:
            inverse = 1.0 / jnp.sum(totals[third], axis=0, keepdims=True)
            inv_ref[third] = jnp.broadcast_to(inverse, inv_ref.shape[1:])
            grad_low = (units.flipped(grad_ref, third).astype(jnp.float32) * inverse).astype(
                jnp.bfloat16
            )
            grad_t_ref[third] = grad_low
        for column, chunk in units.chunks():
            if first < units.count:
                keys = buffer[block_of(place_ref, units.entry(first, column)), units.lanes(first)]
                score = lax.dot_general(keys, query, NT, preferred_element_type=jnp.float32)
                score_ref[first % 2, chunk] = score
                top_new = joined(jnp.maximum, top_new, fold(score, jnp.max))
            if 0 <= second < units.count:
                weight = jnp.exp2(score_ref[second % 2, chunk] * factor - top)
                exp_ref[second, chunk] = weight.astype(jnp.bfloat16)
                total_new = joined(jnp.add, total_new, fold(weight, jnp.sum))
            if 0 <= third:
                acc[block_of(place_ref, units.entry(third, column)), units.lanes(third)] += (
                    lax.dot_general(
                        exp_ref[third, chunk], grad_low, NT, preferred_element_type=jnp.float32
                    )
                )
        tops[first], totals[second] = top_new, total_new
    write_sums(acc, out_refs, tokens, me_tp, None)


def scores_kernel(pieces, units, tokens, place_ref, tp_ref, query_ref, exp_ref, grad_t_ref, inv_ref, *refs):
    count = len(pieces)
    piece_refs = refs[:count]
    ds_ref, buffer = refs[count : count + 2]
    out_refs = refs[count + 2 : count + 6]
    acc, dprob_ref = refs[count + 6 :]
    me_tp = tp_ref[0]
    acc[...] = jnp.zeros_like(acc)
    place_pieces(piece_refs, pieces, tokens, me_tp, buffer)
    deltas = {}
    for step in range(units.count + 2):
        first, second, third = step, step - 1, step - 2
        delta_new = None
        if 0 <= second < units.count:
            delta = jnp.sum(deltas[second], axis=0, keepdims=True) * inv_ref[second, 0:1]
        if 0 <= third:
            query = units.stacked(query_ref, third)
        for column, chunk in units.chunks():
            if first < units.count:
                values = buffer[block_of(place_ref, units.entry(first, column)), units.lanes(first)]
                dprob = jnp.dot(values, grad_t_ref[first], preferred_element_type=jnp.float32)
                dprob_ref[first % 2, chunk] = dprob
                weight = exp_ref[first, chunk].astype(jnp.float32)
                delta_new = joined(jnp.add, delta_new, fold(weight * dprob, jnp.sum))
            if 0 <= second < units.count:
                weight = exp_ref[second, chunk].astype(jnp.float32)
                ds_ref[second, chunk] = (weight * (dprob_ref[second % 2, chunk] - delta)).astype(
                    jnp.bfloat16
                )
            if 0 <= third:
                acc[block_of(place_ref, units.entry(third, column)), units.lanes(third)] += jnp.dot(
                    ds_ref[third, chunk], query, preferred_element_type=jnp.float32
                )
        deltas[first] = delta_new
    write_sums(acc, out_refs, tokens, me_tp, float(HD) ** (-0.5))


def rows_kernel(units, place_ref, exp_ref, ds_ref, inv_ref, keys_ref, values_ref, out_ref, dq_ref, listed):
    scale = float(HD) ** (-0.5)
    for unit in range(units.count):
        slot = unit % 2
        for column, chunk in units.chunks():
            block = block_of(place_ref, units.entry(unit, column))
            listed[2 * slot, chunk] = values_ref[block, units.lanes(unit)]
            listed[2 * slot + 1, chunk] = keys_ref[block, units.lanes(unit)]
        attended = lax.dot_general(
            listed[2 * slot], exp_ref[unit], TN, preferred_element_type=jnp.float32
        )
        attended = (attended * inv_ref[unit, 0:1]).astype(jnp.bfloat16)
        query_grad = lax.dot_general(
            listed[2 * slot + 1], ds_ref[unit], TN, preferred_element_type=jnp.float32
        )
        query_grad = (query_grad * scale).astype(jnp.bfloat16)
        for g, part in enumerate(units.parts(unit)):
            out_ref[units.rows(unit), part] = attended[:, g * BLK : (g + 1) * BLK].T
            dq_ref[units.rows(unit), part] = query_grad[:, g * BLK : (g + 1) * BLK].T


def to_head_groups(rows):
    me = lax.axis_index("tp")
    count = lax.axis_size("tp")
    width = rows.shape[1] // count
    parts = []
    for mask in range(count):
        part = lax.dynamic_slice_in_dim(rows, (me ^ mask) * width, width, 1)
        parts.append(part if mask == 0 else swap(part, "tp", mask))
    return jnp.stack(parts)


def to_quarters(pieces):
    me = lax.axis_index("tp")
    count, quarter, width = pieces.shape
    out = jnp.zeros((quarter, count * width), pieces.dtype)
    for mask in range(count):
        part = pieces[mask] if mask == 0 else swap(pieces[mask], "tp", mask)
        out = lax.dynamic_update_slice(out, part, (0, (me ^ mask) * width))
    return out


def gather_shards(own, after):
    half = own.shape[0] // 2
    started = own if after is None else lax.optimization_barrier((own, after))[0]
    across = swap(started, "ctx", 2)
    along = swap(started, "ctx", 4)
    first = swap(along[:half], "ctx", 2)
    second = swap(across[half:], "ctx", 4)
    near = [own, across, along, first, second]
    far = [swap(part, "ctx", 1) for part in near]
    return near + far


def shard_pieces(count):
    half = count // 2
    near = [(0, 0, count), (2, 0, count), (4, 0, count), (6, 0, half), (6, half, half)]
    return near + [(shard + 1, first, many) for shard, first, many in near]


def sum_shards(near, far3, far12, far0):
    half = near.shape[1] // 2
    got3 = swap(far3, "ctx", 1)
    got12 = swap(far12, "ctx", 1)
    got0 = swap(far0, "ctx", 1)
    diag_a = near[3, :half] + got3[:half]
    diag_b = near[3, half:] + got3[half:]
    from_x = swap(diag_a, "ctx", 2)
    from_y = swap(diag_b, "ctx", 4)
    across_a = near[1, :half] + got12[0, :half]
    along_b = near[2, half:] + got12[1, half:]
    own_a = swap(across_a, "ctx", 2)
    own_b = swap(along_b, "ctx", 4)
    across_b = near[1, half:] + got12[0, half:] + from_y
    along_a = near[2, :half] + got12[1, :half] + from_x
    more_b = swap(across_b, "ctx", 2)
    more_a = swap(along_a, "ctx", 4)
    own = near[0] + got0
    return own + jnp.concatenate([own_a + more_a, own_b + more_b], axis=0)


def dense_plan(queries, key_rows, value_rows, out_grad, block_list):
    tokens = queries.shape[0]
    blocks = tokens // BLK
    shard_total = lax.axis_size("ctx")
    quarters = lax.axis_size("tp")
    width = block_list.shape[1]
    head_width = key_rows.shape[1] // quarters
    heads = head_width // HD
    group = queries.shape[1] // head_width
    rows = shard_total * tokens
    me_ctx = lax.axis_index("ctx")
    me_tp = lax.axis_index("tp").reshape(1)
    places = ((block_list // blocks) ^ me_ctx) * blocks + block_list % blocks
    places = places.reshape(-1)
    quarter = tokens // quarters
    pieces = shard_pieces(quarters)
    units = Units(blocks, width, heads, group)
    list_len = width * BLK
    query_rows = group * BLK
    big = (units.count, list_len, query_rows)

    in_vmem = pl.BlockSpec(memory_space=pltpu.VMEM)
    in_smem = pl.BlockSpec(memory_space=pltpu.SMEM)
    shard_sum = (quarters, quarter, head_width)
    sum_shapes = [
        pltpu.VMEM((shard_total // 2, *shard_sum), jnp.bfloat16),
        pltpu.VMEM(shard_sum, jnp.bfloat16),
        pltpu.VMEM((2, *shard_sum), jnp.bfloat16),
        pltpu.VMEM(shard_sum, jnp.bfloat16),
    ]
    scratch = [
        pltpu.VMEM((rows, head_width), jnp.float32),
        pltpu.VMEM((2, list_len, query_rows), jnp.float32),
    ]
    params = pltpu.CompilerParams(vmem_limit_bytes=16 * 2**20)
    cost = pl.CostEstimate(
        flops=4 * units.count * list_len * query_rows * HD, bytes_accessed=2**24, transcendentals=0
    )

    key_groups = to_head_groups(key_rows)
    keys = gather_shards(key_groups, None)
    value_rows = lax.optimization_barrier((value_rows, key_groups))[0]
    values = gather_shards(to_head_groups(value_rows), (keys[3], keys[4]))

    made = pl.pallas_call(
        functools.partial(probs_kernel, pieces, units, tokens),
        in_specs=[in_smem] * 2 + [in_vmem] * (2 + len(pieces)),
        out_specs=[in_vmem] * 8,
        out_shape=[
            pltpu.VMEM(big, jnp.bfloat16),
            pltpu.VMEM((units.count, HD, query_rows), jnp.bfloat16),
            pltpu.VMEM((units.count, 8, query_rows), jnp.float32),
            pltpu.VMEM((rows, head_width), jnp.bfloat16),
        ]
        + sum_shapes,
        scratch_shapes=scratch,
        compiler_params=params,
        cost_estimate=cost,
        name="probs",
    )(places, me_tp, queries, out_grad, *keys)
    exp_low, grad_t, inverse, keys_in_order = made[:4]
    value_sum = sum_shards(*made[4:])

    made = pl.pallas_call(
        functools.partial(scores_kernel, pieces, units, tokens),
        in_specs=[in_smem] * 2 + [in_vmem] * (4 + len(pieces)),
        out_specs=[in_vmem] * 6,
        out_shape=[pltpu.VMEM(big, jnp.bfloat16), pltpu.VMEM((rows, head_width), jnp.bfloat16)]
        + sum_shapes,
        scratch_shapes=scratch,
        compiler_params=params,
        cost_estimate=cost,
        name="scores",
    )(places, me_tp, queries, exp_low, grad_t, inverse, *values)
    ds_low, values_in_order = made[:2]
    key_sum = sum_shards(*made[2:])

    attended, query_grad = pl.pallas_call(
        functools.partial(rows_kernel, units),
        in_specs=[in_smem] + [in_vmem] * 5,
        out_specs=[in_vmem] * 2,
        out_shape=[jax.ShapeDtypeStruct(queries.shape, jnp.bfloat16)] * 2,
        scratch_shapes=[pltpu.VMEM((4, list_len, HD), jnp.bfloat16)],
        compiler_params=params,
        cost_estimate=cost,
        name="rows",
    )(places, exp_low, ds_low, inverse, keys_in_order, values_in_order)
    return attended, query_grad, to_quarters(key_sum), to_quarters(value_sum)


def solution(mesh):
    dense = mesh.shape["ctx"] == DENSE_SHARDS and mesh.shape["tp"] % 4 == 0
    in_specs = (
        P("ctx", "tp"),
        P(("ctx", "tp"), None),
        P(("ctx", "tp"), None),
        P("ctx", "tp"),
        P("ctx", None),
    )
    out_specs = (P("ctx", "tp"), P("ctx", "tp"), P(("ctx", "tp"), None), P(("ctx", "tp"), None))
    return jax.shard_map(
        dense_plan if dense else sparse_plan,
        mesh=mesh,
        in_specs=in_specs,
        out_specs=out_specs,
        check_vma=False,
    )
```

```python
import functools

import jax
import jax.numpy as jnp
from jax import lax
from jax.experimental import pallas as pl
from jax.experimental.pallas import tpu as pltpu
from jax.sharding import PartitionSpec as P

HD = 128
BLK = 128
GLOB = 2
WIN = 3
RAND = 3


def padded_2(cells, sides, width):
    for axis, dim in sides:
        count = lax.axis_size(axis)
        head = lax.slice_in_dim(cells, 0, width, axis=dim)
        tail = lax.slice_in_dim(cells, cells.shape[dim] - width, cells.shape[dim], axis=dim)
        cells = jnp.concatenate(
            [
                lax.ppermute(tail, axis, [(i, (i + 1) % count) for i in range(count)]),
                cells,
                lax.ppermute(head, axis, [((i + 1) % count, i) for i in range(count)]),
            ],
            axis=dim,
        )
    return cells


def spread(x, axis, root):
    mine = lax.axis_index(axis) == root
    return lax.psum(jnp.where(mine, x, jnp.zeros_like(x)), axis)


def shifted(value, axis, steps):
    count = lax.axis_size(axis)
    pairs = [(source, (source + steps) % count) for source in range(count)]
    return lax.ppermute(value, axis, pairs)


def attend_block(tiles):
    query_tile, grad_tile, keys_tile, values_tile = tiles
    inverse_root = float(HD) ** (-0.5)
    scores = (
        jnp.einsum("qkgd,nkd->kgqn", query_tile, keys_tile, preferred_element_type=jnp.float32)
        * inverse_root
    )
    row_max = jnp.max(scores, axis=-1, keepdims=True)
    logsum = row_max + jnp.log(jnp.sum(jnp.exp(scores - row_max), axis=-1, keepdims=True))
    weights_f = jnp.exp(scores - logsum)
    weights_low = weights_f.astype(jnp.bfloat16)
    attended = jnp.einsum(
        "kgqn,nkd->qkgd", weights_low, values_tile, preferred_element_type=jnp.float32
    ).astype(jnp.bfloat16)
    row_delta = jnp.sum(grad_tile.astype(jnp.float32) * attended.astype(jnp.float32), axis=-1)
    row_delta = jnp.transpose(row_delta, (1, 2, 0))
    dweights = jnp.einsum(
        "qkgd,nkd->kgqn", grad_tile, values_tile, preferred_element_type=jnp.float32
    )
    dscores_low = (weights_f * (dweights - row_delta[..., None])).astype(jnp.bfloat16)
    query_grad = (
        jnp.einsum("kgqn,nkd->qkgd", dscores_low, keys_tile, preferred_element_type=jnp.float32)
        * inverse_root
    ).astype(jnp.bfloat16)
    value_part = jnp.einsum(
        "kgqn,qkgd->nkd", weights_low, grad_tile, preferred_element_type=jnp.float32
    )
    key_part = (
        jnp.einsum("kgqn,qkgd->nkd", dscores_low, query_tile, preferred_element_type=jnp.float32)
        * inverse_root
    )
    return (attended, query_grad, key_part, value_part)


def sparse_plan(queries, key_rows, value_rows, out_grad, block_list):
    tokens_here = queries.shape[0]
    block_count = tokens_here // BLK
    shard_total = lax.axis_size("ctx")
    my_index = lax.axis_index("ctx")
    local_keys, local_values = (
        lax.all_to_all(key_rows, "tp", split_axis=1, concat_axis=0, tiled=True),
        lax.all_to_all(value_rows, "tp", split_axis=1, concat_axis=0, tiled=True),
    )
    head_width = local_keys.shape[1]
    kv_heads = head_width // HD
    both_width = 2 * head_width
    joined = jnp.concatenate([local_keys, local_values], axis=1)
    joined_blocks = joined.reshape(block_count, BLK, both_width)
    padded = padded_2(joined, (("ctx", 0),), BLK)
    padded = padded.reshape(block_count + 2, BLK, both_width)
    window_kv = jnp.stack(
        [padded[0:block_count], padded[1 : block_count + 1], padded[2 : block_count + 2]], axis=1
    )
    global_ids = block_list[0, 0:GLOB]
    global_owner = global_ids // block_count
    global_local = global_ids % block_count
    fetched_list = []
    for column in range(GLOB):
        owned = lax.dynamic_index_in_dim(joined_blocks, global_local[column], 0, keepdims=False)
        fetched_list.append(spread(owned, "ctx", global_owner[column]))
    global_kv = jnp.stack(fetched_list, axis=0)
    random_ids = block_list[:, GLOB + WIN :].reshape(-1)
    ref_count = random_ids.shape[0]
    capacity = (ref_count + shard_total - 1) // shard_total
    slot_count = shard_total * capacity
    ref_owner = random_ids // block_count
    ref_local = random_ids % block_count
    ref_order = jnp.arange(ref_count, dtype=jnp.int32)
    earlier = (ref_owner[:, None] == ref_owner[None, :]) & (ref_order[None, :] < ref_order[:, None])
    ref_rank = jnp.sum(earlier, axis=1)
    ref_slot = ref_owner * capacity + ref_rank
    slot_hit = ref_slot[:, None] == jnp.arange(slot_count, dtype=jnp.int32)[None, :]
    wanted = jnp.sum(jnp.where(slot_hit, ref_local[:, None] + 1, 0), axis=0) - 1
    asked = lax.all_to_all(
        wanted.reshape(shard_total, capacity), "ctx", split_axis=0, concat_axis=0, tiled=True
    )
    valid_ask = asked >= 0
    served = jnp.where(
        valid_ask[:, :, None, None],
        joined_blocks[jnp.maximum(asked, 0)],
        jnp.zeros((), jnp.bfloat16),
    )
    arrived = lax.all_to_all(served, "ctx", split_axis=0, concat_axis=0, tiled=True).reshape(
        slot_count, BLK, both_width
    )
    random_kv = arrived[ref_slot].reshape(block_count, RAND, BLK, both_width)
    list_len = GLOB + WIN + RAND
    global_rep = jnp.broadcast_to(global_kv[None], (block_count, GLOB, BLK, both_width))
    listed_kv = jnp.concatenate([global_rep, window_kv, random_kv], axis=1)
    keys_here = listed_kv[..., :head_width].reshape(block_count, list_len * BLK, kv_heads, HD)
    values_here = listed_kv[..., head_width:].reshape(block_count, list_len * BLK, kv_heads, HD)
    group_size = queries.shape[1] // head_width
    query_tiles = queries.reshape(block_count, BLK, kv_heads, group_size, HD)
    grad_tiles = out_grad.reshape(block_count, BLK, kv_heads, group_size, HD)
    attended, query_grad, key_part, value_part = lax.map(
        attend_block, (query_tiles, grad_tiles, keys_here, values_here)
    )
    grad_kv = jnp.concatenate(
        [
            key_part.reshape(block_count, list_len, BLK, head_width),
            value_part.reshape(block_count, list_len, BLK, head_width),
        ],
        axis=-1,
    )
    window_grad = grad_kv[:, GLOB : GLOB + WIN]
    zero_block = jnp.zeros((1, BLK, both_width), jnp.float32)
    rim_acc = (
        jnp.concatenate([window_grad[:, 0], zero_block, zero_block], axis=0)
        + jnp.concatenate([zero_block, window_grad[:, 1], zero_block], axis=0)
        + jnp.concatenate([zero_block, zero_block, window_grad[:, 2]], axis=0)
    )
    from_left = shifted(rim_acc[block_count + 1].astype(jnp.bfloat16), "ctx", 1).astype(jnp.float32)
    from_right = shifted(rim_acc[0].astype(jnp.bfloat16), "ctx", -1).astype(jnp.float32)
    own_grads = rim_acc[1 : block_count + 1]
    own_grads = own_grads.at[0].add(from_left)
    own_grads = own_grads.at[block_count - 1].add(from_right)
    global_terms = lax.psum(jnp.sum(grad_kv[:, 0:GLOB], axis=0), "ctx")
    global_place = (global_local[:, None] == jnp.arange(block_count, dtype=jnp.int32)[None, :]) & (
        global_owner == my_index
    )[:, None]
    own_grads = own_grads + jnp.einsum(
        "ro,rhn->ohn",
        global_place.astype(jnp.float32),
        global_terms,
        precision=lax.Precision.HIGHEST,
    )
    random_grad = grad_kv[:, GLOB + WIN :].reshape(ref_count, BLK, both_width)
    outgoing = jnp.zeros((slot_count, BLK, both_width), jnp.float32).at[ref_slot].set(random_grad)
    returned = lax.all_to_all(
        outgoing.reshape(shard_total, capacity, BLK, both_width).astype(jnp.bfloat16),
        "ctx",
        split_axis=0,
        concat_axis=0,
        tiled=True,
    ).astype(jnp.float32)
    returned = returned.reshape(slot_count, BLK, both_width)
    slot_place = (
        asked.reshape(slot_count)[:, None] == jnp.arange(block_count, dtype=jnp.int32)[None, :]
    ).astype(jnp.float32)
    own_grads = own_grads + jnp.einsum(
        "sj,sxc->jxc", slot_place, returned, precision=lax.Precision.HIGHEST
    )
    own_grads = own_grads.reshape(tokens_here, both_width).astype(jnp.bfloat16)
    key_grad, value_grad = (
        lax.all_to_all(own_grads[:, :head_width], "tp", split_axis=0, concat_axis=1, tiled=True),
        lax.all_to_all(own_grads[:, head_width:], "tp", split_axis=0, concat_axis=1, tiled=True),
    )
    return (
        attended.reshape(tokens_here, -1),
        query_grad.reshape(tokens_here, -1),
        key_grad,
        value_grad,
    )


LOG2E = 1.4426950408889634
DENSE_SHARDS = 8
VMEM_MIB = 12
NT = (((1,), (1,)), ((), ()))
TN = (((0,), (0,)), ((), ()))


def swap(value, axis, mask):
    count = lax.axis_size(axis)
    return lax.ppermute(value, axis, [(i, i ^ mask) for i in range(count)])


def rows_of(quarter, shard, spot, tokens, me_tp):
    return pl.ds(pl.multiple_of(shard * tokens + (spot ^ me_tp) * quarter, 16), quarter)


def place_pieces(piece_refs, pieces, tokens, me_tp, buffer):
    for ref, (shards, first, spots) in zip(piece_refs, pieces):
        for at in range(ref.shape[0]):
            shard, spot = shards[at // spots], first + at % spots
            buffer[rows_of(ref.shape[1], shard, spot, tokens, me_tp)] = ref[at]


def write_sums(acc, out_refs, tokens, me_tp, scale):
    near_ref, far_ref = out_refs
    for k in range(near_ref.shape[0]):
        for ref, shard in ((far_ref.at[k], 2 * k + 1), (near_ref.at[k], 2 * k)):
            for spot in range(ref.shape[0]):
                part = acc[rows_of(ref.shape[1], shard, spot, tokens, me_tp)]
                if scale is not None:
                    part = part * scale
                ref[spot] = part.astype(ref.dtype)


def block_of(place_ref, entry):
    return pl.ds(pl.multiple_of(place_ref[entry] * BLK, BLK), BLK)


def fold(value, op):
    rows, width = value.shape
    return op(value.reshape(rows // 8, 8, width), axis=0)


def joined(op, total, value):
    return value if total is None else op(total, value)


class Shape:
    def __init__(self, blocks, width, heads, group):
        self.blocks, self.width, self.heads, self.group = blocks, width, heads, group

    def rows(self, row):
        return slice(row * BLK, (row + 1) * BLK)

    def lanes(self, head):
        return slice(head * HD, (head + 1) * HD)

    def parts(self, head):
        first = head * self.group
        return [slice((first + g) * HD, (first + g + 1) * HD) for g in range(self.group)]

    def wide(self, head):
        return slice(head * self.group * HD, (head + 1) * self.group * HD)

    def chunks(self):
        return [(c, slice(c * BLK, (c + 1) * BLK)) for c in range(self.width)]

    def entry(self, row, column):
        return row * self.width + column

    def stacked(self, ref, row, head):
        return jnp.concatenate([ref[self.rows(row), part] for part in self.parts(head)], axis=0)

    def flipped(self, ref, row, head):
        return jnp.concatenate([ref[self.rows(row), part].T for part in self.parts(head)], axis=1)


def exps_kernel(head, pieces, dims, tokens, place_ref, tp_ref, query_ref, grad_ref, *refs):
    query, grad, score_ref, sems = refs[-4:]
    query_copy = pltpu.make_async_copy(query_ref.at[:, dims.wide(head)], query, sems.at[0])
    grad_copy = pltpu.make_async_copy(grad_ref.at[:, dims.wide(head)], grad, sems.at[1])
    query_copy.start()
    grad_copy.start()
    if pieces:
        count = len(pieces)
        exp_ref, grad_t_ref, inv_ref, buffer = refs[count:-4]
        place_pieces(refs[:count], pieces, tokens, tp_ref[0], buffer)
    else:
        buffer, exp_ref, grad_t_ref, inv_ref = refs[:-4]
    query_copy.wait()
    grad_copy.wait()
    factor = LOG2E * float(HD) ** (-0.5)
    lanes = dims.lanes(head)
    tops = {}
    for step in range(dims.blocks + 1):
        first, second = step, step - 1
        top_new = total = None
        if first < dims.blocks:
            stacked = dims.stacked(query, first, 0)
        if 0 <= second:
            top = jnp.max(tops[second], axis=0, keepdims=True) * factor
        for column, chunk in dims.chunks():
            if first < dims.blocks:
                keys = buffer[block_of(place_ref, dims.entry(first, column)), lanes]
                score = lax.dot_general(keys, stacked, NT, preferred_element_type=jnp.float32)
                score_ref[first % 2, chunk] = score
                top_new = joined(jnp.maximum, top_new, fold(score, jnp.max))
            if 0 <= second:
                weight = jnp.exp2(score_ref[second % 2, chunk] * factor - top)
                exp_ref[second, chunk] = weight.astype(jnp.bfloat16)
                total = joined(jnp.add, total, fold(weight, jnp.sum))
        tops[first] = top_new
        if 0 <= second:
            inverse = 1.0 / jnp.sum(total, axis=0, keepdims=True)
            inv_ref[second] = jnp.broadcast_to(inverse, inv_ref.shape[1:])
            grad_t = dims.flipped(grad, second, 0).astype(jnp.float32)
            grad_t_ref[second] = (grad_t * inverse).astype(jnp.bfloat16)


def values_kernel(dims, tokens, place_ref, tp_ref, *refs):
    exp_refs, grad_t_refs = refs[: dims.heads], refs[dims.heads : 2 * dims.heads]
    out_refs, acc = refs[2 * dims.heads : -1], refs[-1]
    acc[...] = jnp.zeros_like(acc)
    for row in range(dims.blocks):
        for head in range(dims.heads):
            for column, chunk in dims.chunks():
                acc[block_of(place_ref, dims.entry(row, column)), dims.lanes(head)] += (
                    lax.dot_general(
                        exp_refs[head][row, chunk],
                        grad_t_refs[head][row],
                        NT,
                        preferred_element_type=jnp.float32,
                    )
                )
    write_sums(acc, out_refs, tokens, tp_ref[0], None)


def add_keys(acc, dims, place_ref, row, head, ds_ref, query):
    stacked = dims.stacked(query, row, head)
    for column, chunk in dims.chunks():
        acc[block_of(place_ref, dims.entry(row, column)), dims.lanes(head)] += jnp.dot(
            ds_ref[row, chunk], stacked, preferred_element_type=jnp.float32
        )


def score_rows(head, dims, place_ref, exp_ref, grad_t_ref, inv_ref, buffer, ds_ref, dprob_ref, then):
    lanes = dims.lanes(head)
    deltas = {}
    for step in range(dims.blocks + 1):
        first, second = step, step - 1
        delta_new = None
        if 0 <= second:
            delta = jnp.sum(deltas[second], axis=0, keepdims=True) * inv_ref[second, 0:1]
        for column, chunk in dims.chunks():
            if first < dims.blocks:
                values = buffer[block_of(place_ref, dims.entry(first, column)), lanes]
                dprob = jnp.dot(values, grad_t_ref[first], preferred_element_type=jnp.float32)
                dprob_ref[first % 2, chunk] = dprob
                weight = exp_ref[first, chunk].astype(jnp.float32)
                delta_new = joined(jnp.add, delta_new, fold(weight * dprob, jnp.sum))
            if 0 <= second:
                weight = exp_ref[second, chunk].astype(jnp.float32)
                ds_ref[second, chunk] = (weight * (dprob_ref[second % 2, chunk] - delta)).astype(
                    jnp.bfloat16
                )
        then(step - 1)
        deltas[first] = delta_new


def scores_kernel(head, pieces, dims, tokens, place_ref, tp_ref, exp_ref, grad_t_ref, inv_ref, *refs):
    count = len(pieces)
    ds_ref, buffer, flag_ref, dprob_ref = refs[count:]
    flag_ref[...] = jnp.zeros_like(flag_ref)
    place_pieces(refs[:count], pieces, tokens, tp_ref[0], buffer)
    score_rows(head, dims, place_ref, exp_ref, grad_t_ref, inv_ref, buffer, ds_ref, dprob_ref, lambda row: None)


def keys_kernel(dims, tokens, place_ref, tp_ref, exp_ref, grad_t_ref, inv_ref, buffer, *refs):
    done_refs, query_ref = refs[: dims.heads - 1], refs[dims.heads - 1]
    ds_ref, *out_refs, acc, dprob_ref, query, sem = refs[dims.heads :]
    query_copy = pltpu.make_async_copy(query_ref, query, sem)
    query_copy.start()
    acc[...] = jnp.zeros_like(acc)
    query_copy.wait()

    def then(row):
        if row < 0:
            return
        for head, done_ref in enumerate(done_refs):
            add_keys(acc, dims, place_ref, row, head, done_ref, query)
        add_keys(acc, dims, place_ref, row, dims.heads - 1, ds_ref, query)

    score_rows(dims.heads - 1, dims, place_ref, exp_ref, grad_t_ref, inv_ref, buffer, ds_ref, dprob_ref, then)
    write_sums(acc, out_refs, tokens, tp_ref[0], float(HD) ** (-0.5))


def rows_kernel(dims, scale, place_ref, buffer_ref, *refs):
    weight_refs, inv_refs = refs[: dims.heads], refs[dims.heads : -2]
    out_ref, listed = refs[-2:]
    for row in range(dims.blocks):
        for head in range(dims.heads):
            for column, chunk in dims.chunks():
                block = block_of(place_ref, dims.entry(row, column))
                listed[head, chunk] = buffer_ref[block, dims.lanes(head)]
            result = lax.dot_general(
                listed[head], weight_refs[head][row], TN, preferred_element_type=jnp.float32
            )
            if scale is None:
                result = result * inv_refs[head][row, 0:1]
            else:
                result = result * scale
            result = result.astype(jnp.bfloat16)
            for g, part in enumerate(dims.parts(head)):
                out_ref[dims.rows(row), part] = result[:, g * BLK : (g + 1) * BLK].T


def to_head_groups(rows):
    me = lax.axis_index("tp")
    count = lax.axis_size("tp")
    width = rows.shape[1] // count
    parts = []
    for mask in range(count):
        part = lax.dynamic_slice_in_dim(rows, (me ^ mask) * width, width, 1)
        parts.append(part if mask == 0 else swap(part, "tp", mask))
    return jnp.stack(parts)


def to_quarters(pieces):
    me = lax.axis_index("tp")
    count, quarter, width = pieces.shape
    out = jnp.zeros((quarter, count * width), pieces.dtype)
    for mask in range(count):
        part = pieces[mask] if mask == 0 else swap(pieces[mask], "tp", mask)
        out = lax.dynamic_update_slice(out, part, (0, (me ^ mask) * width))
    return out


def cut(*values):
    return lax.optimization_barrier(values)


def held_until(value, *others):
    return lax.optimization_barrier((value, *others))[0]


def with_near(own):
    return swap(own, "ctx", 2), swap(own, "ctx", 4)


def with_diagonal(along_half, across_half):
    return swap(along_half, "ctx", 2), swap(across_half, "ctx", 4)


def to_diagonal(near, got):
    half = near.shape[1] // 2
    to_x = jnp.stack([near[3, :half] + got[3, :half], near[1, :half] + got[1, :half]])
    to_y = jnp.stack([near[3, half:] + got[3, half:], near[2, half:] + got[2, half:]])
    return to_x, to_y


def send_near(near, got, from_x, from_y):
    half = near.shape[1] // 2
    more_b = swap(near[1, half:] + got[1, half:] + from_y[0], "ctx", 2)
    more_a = swap(near[2, :half] + got[2, :half] + from_x[0], "ctx", 4)
    return more_a, more_b


def total_own(near, got, from_x, from_y, more_a, more_b):
    own = near[0] + got[0]
    return own + jnp.concatenate([from_x[1] + more_a, from_y[1] + more_b], axis=0)


def dense_plan(queries, key_rows, value_rows, out_grad, block_list):
    tokens = queries.shape[0]
    blocks = tokens // BLK
    shard_total = lax.axis_size("ctx")
    quarters = lax.axis_size("tp")
    width = block_list.shape[1]
    head_width = key_rows.shape[1] // quarters
    heads = head_width // HD
    group = queries.shape[1] // head_width
    rows = shard_total * tokens
    me_ctx = lax.axis_index("ctx")
    me_tp = lax.axis_index("tp").reshape(1)
    places = ((block_list // blocks) ^ me_ctx) * blocks + block_list % blocks
    places = places.reshape(-1)
    quarter = tokens // quarters
    half = quarters // 2
    pieces = [((shard,), 0, quarters) for shard in (0, 2, 4)]
    pieces += [((6,), 0, half), ((6,), half, half), ((1, 3, 5), 0, quarters)]
    pieces += [((7,), 0, half), ((7,), half, half)]
    dims = Shape(blocks, width, heads, group)
    list_len = width * BLK
    query_rows = group * BLK
    bf16 = jnp.bfloat16

    in_vmem = pl.BlockSpec(memory_space=pltpu.VMEM)
    in_smem = pl.BlockSpec(memory_space=pltpu.SMEM)
    in_any = pl.BlockSpec(memory_space=pl.ANY)
    shape = jax.ShapeDtypeStruct
    sums = [shape((shard_total // 2, quarters, quarter, head_width), bf16)] * 2
    stash = shape((blocks, list_len, query_rows), bf16)
    grads = shape((blocks, HD, query_rows), bf16)
    inverses = shape((blocks, 8, query_rows), jnp.float32)
    ordered = shape((rows, head_width), bf16)
    flat = shape(queries.shape, bf16)
    flag = shape((8, HD), jnp.float32)
    two_rows = pltpu.VMEM((2, list_len, query_rows), jnp.float32)
    total = pltpu.VMEM((rows, head_width), jnp.float32)
    listed = pltpu.VMEM((heads, list_len, HD), bf16)
    wide = pltpu.VMEM((tokens, group * HD), bf16)
    whole = pltpu.VMEM(queries.shape, bf16)
    sem = pltpu.SemaphoreType.DMA

    def call(name, kernel, outs, scratch, scalars, operands):
        return pl.pallas_call(
            kernel,
            in_specs=[in_smem] * len(scalars) + [in_any if x is queries or x is out_grad else in_vmem for x in operands],
            out_specs=[in_vmem] * len(outs),
            out_shape=outs,
            scratch_shapes=scratch,
            compiler_params=pltpu.CompilerParams(vmem_limit_bytes=VMEM_MIB * 2**20),
            cost_estimate=pl.CostEstimate(flops=2**32, bytes_accessed=2**20, transcendentals=0),
            name=name,
        )(*scalars, *operands)

    key_own = to_head_groups(key_rows)
    key_x, key_y = with_near(key_own)
    value_own = to_head_groups(value_rows)
    key_x, key_y, key_own, value_own = cut(key_x, key_y, key_own, value_own)
    key_y1, key_x2, key_three = cut(
        key_y[:half], key_x[half:], jnp.concatenate([key_own, key_x, key_y])
    )
    key_d1, key_d2 = with_diagonal(key_y1, key_x2)
    key_d1, key_d2, key_three = cut(key_d1, key_d2, key_three)
    keys = [key_own, key_x, key_y, key_d1, key_d2]
    keys += [swap(part, "ctx", 1) for part in (key_three, key_d1, key_d2)]
    value_x, value_y = with_near(held_until(value_own, key_d1))

    rows_scratch = [wide, wide, two_rows, sem((2,))]
    exp_0, grad_0, inverse_0, keys_in_order = call(
        "exps_0", functools.partial(exps_kernel, 0, pieces, dims, tokens),
        [stash, grads, inverses, ordered], rows_scratch, (places, me_tp), (queries, out_grad, *keys),
    )
    value_x, value_y, inverse_0 = cut(value_x, value_y, inverse_0)
    value_y1, value_x2, value_three, places_1 = cut(
        value_y[:half], value_x[half:], jnp.concatenate([value_own, value_x, value_y]), places
    )
    value_d1, value_d2 = with_diagonal(value_y1, value_x2)
    value_far = swap(value_three, "ctx", 1)
    exps, grad_ts, inverse = [exp_0], [grad_0], [inverse_0]
    for head in range(1, heads):
        made = call(
            "exps", functools.partial(exps_kernel, head, [], dims, tokens),
            [stash, grads, inverses], rows_scratch, (places_1, me_tp),
            (queries, out_grad, keys_in_order),
        )
        for kept, new in zip((exps, grad_ts, inverse), made):
            kept.append(new)
    value_d1, value_d2, value_far, inverse[-1] = cut(value_d1, value_d2, value_far, inverse[-1])
    values = [value_own, value_x, value_y, value_d1, value_d2, value_far]
    values += [swap(part, "ctx", 1) for part in (value_d1, value_d2)]
    value_near, value_away = call(
        "value_sums", functools.partial(values_kernel, dims, tokens),
        sums, [total], (held_until(places, inverse[-1]), me_tp), (*exps, *grad_ts),
    )
    value_near, value_away, places_2, *values[-2:] = cut(value_near, value_away, places, *values[-2:])
    value_got = swap(value_away, "ctx", 1)
    ds, token = [], None
    for head in range(heads - 1):
        made, values_in_order, token = call(
            "scores", functools.partial(scores_kernel, head, pieces, dims, tokens),
            [stash, ordered, flag], [two_rows], (places_2, me_tp),
            (exps[head], grad_ts[head], inverse[head], *values),
        )
        ds.append(made)
    value_got, token = cut(value_got, token)
    to_x, to_y = to_diagonal(value_near, value_got)
    to_x, to_y, places_3 = cut(to_x, to_y, held_until(places, token))
    value_first = swap(to_x, "ctx", 2), swap(to_y, "ctx", 4)
    made, key_near, key_away = call(
        "key_sums", functools.partial(keys_kernel, dims, tokens),
        [stash, *sums], [total, two_rows, whole, sem], (places_3, me_tp),
        (exps[-1], grad_ts[-1], inverse[-1], values_in_order, *ds, queries),
    )
    ds.append(made)
    key_near, key_away, places_4, *value_first = cut(key_near, key_away, places, *value_first)
    key_got = swap(key_away, "ctx", 1)
    value_more = send_near(value_near, value_got, *value_first)
    [attended] = call(
        "attended", functools.partial(rows_kernel, dims, None),
        [flat], [listed], (places_4,), (values_in_order, *exps, *inverse),
    )
    key_got, attended, *value_more = cut(key_got, attended, *value_more)
    value_sum = total_own(value_near, value_got, *value_first, *value_more)
    to_x, to_y = to_diagonal(key_near, key_got)
    to_x, to_y, places_5, value_sum = cut(to_x, to_y, places, value_sum)
    key_first = swap(to_x, "ctx", 2), swap(to_y, "ctx", 4)
    value_grad = to_quarters(value_sum)
    [query_grad] = call(
        "query_grad", functools.partial(rows_kernel, dims, float(HD) ** (-0.5)),
        [flat], [listed], (places_5,), (keys_in_order, *ds),
    )
    query_grad, *key_first = cut(query_grad, *key_first)
    key_more = send_near(key_near, key_got, *key_first)
    key_sum = total_own(key_near, key_got, *key_first, *key_more)
    return attended, query_grad, to_quarters(key_sum), value_grad


def solution(mesh):
    dense = mesh.shape["ctx"] == DENSE_SHARDS and mesh.shape["tp"] % 4 == 0
    in_specs = (
        P("ctx", "tp"),
        P(("ctx", "tp"), None),
        P(("ctx", "tp"), None),
        P("ctx", "tp"),
        P("ctx", None),
    )
    out_specs = (P("ctx", "tp"), P("ctx", "tp"), P(("ctx", "tp"), None), P(("ctx", "tp"), None))
    return jax.shard_map(
        dense_plan if dense else sparse_plan,
        mesh=mesh,
        in_specs=in_specs,
        out_specs=out_specs,
        check_vma=False,
    )
```

```python
import functools

import jax
import jax.numpy as jnp
from jax import lax
from jax.experimental import pallas as pl
from jax.experimental.pallas import tpu as pltpu
from jax.sharding import PartitionSpec as P

HD = 128
BLK = 128
GLOB = 2
WIN = 3
RAND = 3


def padded_2(cells, sides, width):
    for axis, dim in sides:
        count = lax.axis_size(axis)
        head = lax.slice_in_dim(cells, 0, width, axis=dim)
        tail = lax.slice_in_dim(cells, cells.shape[dim] - width, cells.shape[dim], axis=dim)
        cells = jnp.concatenate(
            [
                lax.ppermute(tail, axis, [(i, (i + 1) % count) for i in range(count)]),
                cells,
                lax.ppermute(head, axis, [((i + 1) % count, i) for i in range(count)]),
            ],
            axis=dim,
        )
    return cells


def spread(x, axis, root):
    mine = lax.axis_index(axis) == root
    return lax.psum(jnp.where(mine, x, jnp.zeros_like(x)), axis)


def shifted(value, axis, steps):
    count = lax.axis_size(axis)
    pairs = [(source, (source + steps) % count) for source in range(count)]
    return lax.ppermute(value, axis, pairs)


def attend_block(tiles):
    query_tile, grad_tile, keys_tile, values_tile = tiles
    inverse_root = float(HD) ** (-0.5)
    scores = (
        jnp.einsum("qkgd,nkd->kgqn", query_tile, keys_tile, preferred_element_type=jnp.float32)
        * inverse_root
    )
    row_max = jnp.max(scores, axis=-1, keepdims=True)
    logsum = row_max + jnp.log(jnp.sum(jnp.exp(scores - row_max), axis=-1, keepdims=True))
    weights_f = jnp.exp(scores - logsum)
    weights_low = weights_f.astype(jnp.bfloat16)
    attended = jnp.einsum(
        "kgqn,nkd->qkgd", weights_low, values_tile, preferred_element_type=jnp.float32
    ).astype(jnp.bfloat16)
    row_delta = jnp.sum(grad_tile.astype(jnp.float32) * attended.astype(jnp.float32), axis=-1)
    row_delta = jnp.transpose(row_delta, (1, 2, 0))
    dweights = jnp.einsum(
        "qkgd,nkd->kgqn", grad_tile, values_tile, preferred_element_type=jnp.float32
    )
    dscores_low = (weights_f * (dweights - row_delta[..., None])).astype(jnp.bfloat16)
    query_grad = (
        jnp.einsum("kgqn,nkd->qkgd", dscores_low, keys_tile, preferred_element_type=jnp.float32)
        * inverse_root
    ).astype(jnp.bfloat16)
    value_part = jnp.einsum(
        "kgqn,qkgd->nkd", weights_low, grad_tile, preferred_element_type=jnp.float32
    )
    key_part = (
        jnp.einsum("kgqn,qkgd->nkd", dscores_low, query_tile, preferred_element_type=jnp.float32)
        * inverse_root
    )
    return (attended, query_grad, key_part, value_part)


def sparse_plan(queries, key_rows, value_rows, out_grad, block_list):
    tokens_here = queries.shape[0]
    block_count = tokens_here // BLK
    shard_total = lax.axis_size("ctx")
    my_index = lax.axis_index("ctx")
    local_keys, local_values = (
        lax.all_to_all(key_rows, "tp", split_axis=1, concat_axis=0, tiled=True),
        lax.all_to_all(value_rows, "tp", split_axis=1, concat_axis=0, tiled=True),
    )
    head_width = local_keys.shape[1]
    kv_heads = head_width // HD
    both_width = 2 * head_width
    joined = jnp.concatenate([local_keys, local_values], axis=1)
    joined_blocks = joined.reshape(block_count, BLK, both_width)
    padded = padded_2(joined, (("ctx", 0),), BLK)
    padded = padded.reshape(block_count + 2, BLK, both_width)
    window_kv = jnp.stack(
        [padded[0:block_count], padded[1 : block_count + 1], padded[2 : block_count + 2]], axis=1
    )
    global_ids = block_list[0, 0:GLOB]
    global_owner = global_ids // block_count
    global_local = global_ids % block_count
    fetched_list = []
    for column in range(GLOB):
        owned = lax.dynamic_index_in_dim(joined_blocks, global_local[column], 0, keepdims=False)
        fetched_list.append(spread(owned, "ctx", global_owner[column]))
    global_kv = jnp.stack(fetched_list, axis=0)
    random_ids = block_list[:, GLOB + WIN :].reshape(-1)
    ref_count = random_ids.shape[0]
    capacity = (ref_count + shard_total - 1) // shard_total
    slot_count = shard_total * capacity
    ref_owner = random_ids // block_count
    ref_local = random_ids % block_count
    ref_order = jnp.arange(ref_count, dtype=jnp.int32)
    earlier = (ref_owner[:, None] == ref_owner[None, :]) & (ref_order[None, :] < ref_order[:, None])
    ref_rank = jnp.sum(earlier, axis=1)
    ref_slot = ref_owner * capacity + ref_rank
    slot_hit = ref_slot[:, None] == jnp.arange(slot_count, dtype=jnp.int32)[None, :]
    wanted = jnp.sum(jnp.where(slot_hit, ref_local[:, None] + 1, 0), axis=0) - 1
    asked = lax.all_to_all(
        wanted.reshape(shard_total, capacity), "ctx", split_axis=0, concat_axis=0, tiled=True
    )
    valid_ask = asked >= 0
    served = jnp.where(
        valid_ask[:, :, None, None],
        joined_blocks[jnp.maximum(asked, 0)],
        jnp.zeros((), jnp.bfloat16),
    )
    arrived = lax.all_to_all(served, "ctx", split_axis=0, concat_axis=0, tiled=True).reshape(
        slot_count, BLK, both_width
    )
    random_kv = arrived[ref_slot].reshape(block_count, RAND, BLK, both_width)
    list_len = GLOB + WIN + RAND
    global_rep = jnp.broadcast_to(global_kv[None], (block_count, GLOB, BLK, both_width))
    listed_kv = jnp.concatenate([global_rep, window_kv, random_kv], axis=1)
    keys_here = listed_kv[..., :head_width].reshape(block_count, list_len * BLK, kv_heads, HD)
    values_here = listed_kv[..., head_width:].reshape(block_count, list_len * BLK, kv_heads, HD)
    group_size = queries.shape[1] // head_width
    query_tiles = queries.reshape(block_count, BLK, kv_heads, group_size, HD)
    grad_tiles = out_grad.reshape(block_count, BLK, kv_heads, group_size, HD)
    attended, query_grad, key_part, value_part = lax.map(
        attend_block, (query_tiles, grad_tiles, keys_here, values_here)
    )
    grad_kv = jnp.concatenate(
        [
            key_part.reshape(block_count, list_len, BLK, head_width),
            value_part.reshape(block_count, list_len, BLK, head_width),
        ],
        axis=-1,
    )
    window_grad = grad_kv[:, GLOB : GLOB + WIN]
    zero_block = jnp.zeros((1, BLK, both_width), jnp.float32)
    rim_acc = (
        jnp.concatenate([window_grad[:, 0], zero_block, zero_block], axis=0)
        + jnp.concatenate([zero_block, window_grad[:, 1], zero_block], axis=0)
        + jnp.concatenate([zero_block, zero_block, window_grad[:, 2]], axis=0)
    )
    from_left = shifted(rim_acc[block_count + 1].astype(jnp.bfloat16), "ctx", 1).astype(jnp.float32)
    from_right = shifted(rim_acc[0].astype(jnp.bfloat16), "ctx", -1).astype(jnp.float32)
    own_grads = rim_acc[1 : block_count + 1]
    own_grads = own_grads.at[0].add(from_left)
    own_grads = own_grads.at[block_count - 1].add(from_right)
    global_terms = lax.psum(jnp.sum(grad_kv[:, 0:GLOB], axis=0), "ctx")
    global_place = (global_local[:, None] == jnp.arange(block_count, dtype=jnp.int32)[None, :]) & (
        global_owner == my_index
    )[:, None]
    own_grads = own_grads + jnp.einsum(
        "ro,rhn->ohn",
        global_place.astype(jnp.float32),
        global_terms,
        precision=lax.Precision.HIGHEST,
    )
    random_grad = grad_kv[:, GLOB + WIN :].reshape(ref_count, BLK, both_width)
    outgoing = jnp.zeros((slot_count, BLK, both_width), jnp.float32).at[ref_slot].set(random_grad)
    returned = lax.all_to_all(
        outgoing.reshape(shard_total, capacity, BLK, both_width).astype(jnp.bfloat16),
        "ctx",
        split_axis=0,
        concat_axis=0,
        tiled=True,
    ).astype(jnp.float32)
    returned = returned.reshape(slot_count, BLK, both_width)
    slot_place = (
        asked.reshape(slot_count)[:, None] == jnp.arange(block_count, dtype=jnp.int32)[None, :]
    ).astype(jnp.float32)
    own_grads = own_grads + jnp.einsum(
        "sj,sxc->jxc", slot_place, returned, precision=lax.Precision.HIGHEST
    )
    own_grads = own_grads.reshape(tokens_here, both_width).astype(jnp.bfloat16)
    key_grad, value_grad = (
        lax.all_to_all(own_grads[:, :head_width], "tp", split_axis=0, concat_axis=1, tiled=True),
        lax.all_to_all(own_grads[:, head_width:], "tp", split_axis=0, concat_axis=1, tiled=True),
    )
    return (
        attended.reshape(tokens_here, -1),
        query_grad.reshape(tokens_here, -1),
        key_grad,
        value_grad,
    )


LOG2E = 1.4426950408889634
DENSE_SHARDS = 8
VMEM_MIB = 8
NT = (((1,), (1,)), ((), ()))
TN = (((0,), (0,)), ((), ()))


def swap(value, axis, mask):
    count = lax.axis_size(axis)
    return lax.ppermute(value, axis, [(i, i ^ mask) for i in range(count)])


def rows_of(quarter, shard, spot, tokens, me_tp):
    return pl.ds(pl.multiple_of(shard * tokens + (spot ^ me_tp) * quarter, 16), quarter)


def place_pieces(piece_refs, pieces, tokens, me_tp, buffer):
    for ref, (shards, first, spots) in zip(piece_refs, pieces):
        for at in range(ref.shape[0]):
            shard, spot = shards[at // spots], first + at % spots
            buffer[rows_of(ref.shape[1], shard, spot, tokens, me_tp)] = ref[at]


def write_sums(acc, out_refs, tokens, me_tp, scale):
    near_ref, far_ref = out_refs
    for k in range(near_ref.shape[0]):
        for ref, shard in ((far_ref.at[k], 2 * k + 1), (near_ref.at[k], 2 * k)):
            for spot in range(ref.shape[0]):
                part = acc[rows_of(ref.shape[1], shard, spot, tokens, me_tp)]
                if scale is not None:
                    part = part * scale
                ref[spot] = part.astype(ref.dtype)


def block_of(place_ref, entry):
    return pl.ds(pl.multiple_of(place_ref[entry] * BLK, BLK), BLK)


def fold(value, op):
    rows, width = value.shape
    return op(value.reshape(rows // 8, 8, width), axis=0)


def joined(op, total, value):
    return value if total is None else op(total, value)


class Shape:
    def __init__(self, blocks, width, heads, group):
        self.blocks, self.width, self.heads, self.group = blocks, width, heads, group

    def rows(self, row):
        return slice(row * BLK, (row + 1) * BLK)

    def lanes(self, head):
        return slice(head * HD, (head + 1) * HD)

    def parts(self, head):
        first = head * self.group
        return [slice((first + g) * HD, (first + g + 1) * HD) for g in range(self.group)]

    def wide(self, head):
        return slice(head * self.group * HD, (head + 1) * self.group * HD)

    def chunks(self):
        return [(c, slice(c * BLK, (c + 1) * BLK)) for c in range(self.width)]

    def entry(self, row, column):
        return row * self.width + column

    def stacked(self, ref, row, head):
        return jnp.concatenate([ref[self.rows(row), part] for part in self.parts(head)], axis=0)

    def flipped(self, ref, row, head):
        return jnp.concatenate([ref[self.rows(row), part].T for part in self.parts(head)], axis=1)


def first_exps_kernel(pieces, dims, tokens, place_ref, tp_ref, query_hbm, grad_hbm, *refs):
    count = len(pieces)
    exp_ref, grad_t_ref, inv_ref, buffer, query, grad, score_ref, sems = refs[count:]
    copies = []
    for head in range(dims.heads):
        for source, target in ((query_hbm, query), (grad_hbm, grad)):
            lanes = dims.wide(head)
            copies.append(
                pltpu.make_async_copy(source.at[:, lanes], target.at[:, lanes], sems.at[len(copies)])
            )
            copies[-1].start()
    place_pieces(refs[:count], pieces, tokens, tp_ref[0], buffer)
    copies[0].wait()
    copies[1].wait()
    exps_kernel(0, dims, place_ref, query, grad, buffer, exp_ref, grad_t_ref, inv_ref, score_ref)
    for copy in copies[2:]:
        copy.wait()


def exps_kernel(head, dims, place_ref, query, grad, buffer, exp_ref, grad_t_ref, inv_ref, score_ref):
    factor = LOG2E * float(HD) ** (-0.5)
    lanes = dims.lanes(head)
    tops = {}
    for step in range(dims.blocks + 1):
        first, second = step, step - 1
        top_new = total = None
        if first < dims.blocks:
            stacked = dims.stacked(query, first, head)
        if 0 <= second:
            top = jnp.max(tops[second], axis=0, keepdims=True) * factor
        for column, chunk in dims.chunks():
            if first < dims.blocks:
                keys = buffer[block_of(place_ref, dims.entry(first, column)), lanes]
                score = lax.dot_general(keys, stacked, NT, preferred_element_type=jnp.float32)
                score_ref[first % 2, chunk] = score
                top_new = joined(jnp.maximum, top_new, fold(score, jnp.max))
            if 0 <= second:
                weight = jnp.exp2(score_ref[second % 2, chunk] * factor - top)
                exp_ref[second, chunk] = weight.astype(jnp.bfloat16)
                total = joined(jnp.add, total, fold(weight, jnp.sum))
        tops[first] = top_new
        if 0 <= second:
            inverse = 1.0 / jnp.sum(total, axis=0, keepdims=True)
            inv_ref[second] = jnp.broadcast_to(inverse, inv_ref.shape[1:])
            grad_t = dims.flipped(grad, second, head).astype(jnp.float32)
            grad_t_ref[second] = (grad_t * inverse).astype(jnp.bfloat16)


def values_kernel(dims, tokens, place_ref, tp_ref, *refs):
    exp_refs, grad_t_refs = refs[: dims.heads], refs[dims.heads : 2 * dims.heads]
    out_refs, acc = refs[2 * dims.heads : -1], refs[-1]
    acc[...] = jnp.zeros_like(acc)
    for row in range(dims.blocks):
        for head in range(dims.heads):
            for column, chunk in dims.chunks():
                acc[block_of(place_ref, dims.entry(row, column)), dims.lanes(head)] += (
                    lax.dot_general(
                        exp_refs[head][row, chunk],
                        grad_t_refs[head][row],
                        NT,
                        preferred_element_type=jnp.float32,
                    )
                )
    write_sums(acc, out_refs, tokens, tp_ref[0], None)


def add_keys(acc, dims, place_ref, row, head, ds_ref, query):
    stacked = dims.stacked(query, row, head)
    for column, chunk in dims.chunks():
        acc[block_of(place_ref, dims.entry(row, column)), dims.lanes(head)] += jnp.dot(
            ds_ref[row, chunk], stacked, preferred_element_type=jnp.float32
        )


def score_rows(head, dims, place_ref, exp_ref, grad_t_ref, inv_ref, buffer, out_ref, ds_ref, listed, then):
    lanes = dims.lanes(head)
    for row in range(dims.blocks):
        slot = row % 2
        for column, chunk in dims.chunks():
            listed[slot, chunk] = buffer[block_of(place_ref, dims.entry(row, column)), lanes]
        attended = lax.dot_general(
            listed[slot], exp_ref[row], TN, preferred_element_type=jnp.float32
        )
        attended = (attended * inv_ref[row, 0:1]).astype(jnp.bfloat16)
        grad_t = grad_t_ref[row]
        delta = jnp.sum(
            grad_t.astype(jnp.float32) * attended.astype(jnp.float32), axis=0, keepdims=True
        )
        for g, part in enumerate(dims.parts(0)):
            out_ref[dims.rows(row), part] = attended[:, g * BLK : (g + 1) * BLK].T
        for column, chunk in dims.chunks():
            dprob = jnp.dot(listed[slot, chunk], grad_t, preferred_element_type=jnp.float32)
            weight = exp_ref[row, chunk].astype(jnp.float32)
            ds_ref[row, chunk] = (weight * (dprob - delta)).astype(jnp.bfloat16)
        then(row)


def scores_kernel(head, pieces, dims, tokens, place_ref, tp_ref, exp_ref, grad_t_ref, inv_ref, *refs):
    count = len(pieces)
    out_ref, ds_ref, buffer, flag_ref, listed = refs[count:]
    flag_ref[...] = jnp.zeros_like(flag_ref)
    place_pieces(refs[:count], pieces, tokens, tp_ref[0], buffer)
    score_rows(
        head, dims, place_ref, exp_ref, grad_t_ref, inv_ref, buffer, out_ref, ds_ref, listed,
        lambda row: None,
    )


def keys_kernel(dims, tokens, place_ref, tp_ref, exp_ref, grad_t_ref, inv_ref, buffer, *refs):
    done_refs, query = refs[: dims.heads - 1], refs[dims.heads - 1]
    out_ref, ds_ref, *sum_refs, acc, listed = refs[dims.heads :]
    acc[...] = jnp.zeros_like(acc)

    def then(row):
        for head, done_ref in enumerate(done_refs):
            add_keys(acc, dims, place_ref, row, head, done_ref, query)
        add_keys(acc, dims, place_ref, row, dims.heads - 1, ds_ref, query)

    score_rows(
        dims.heads - 1, dims, place_ref, exp_ref, grad_t_ref, inv_ref, buffer, out_ref, ds_ref,
        listed, then,
    )
    write_sums(acc, sum_refs, tokens, tp_ref[0], float(HD) ** (-0.5))


def rows_kernel(dims, place_ref, buffer_ref, *refs):
    weight_refs = refs[: dims.heads]
    out_ref, flag_ref, listed = refs[dims.heads :]
    flag_ref[...] = jnp.zeros_like(flag_ref)
    for row in range(dims.blocks):
        for head in range(dims.heads):
            for column, chunk in dims.chunks():
                block = block_of(place_ref, dims.entry(row, column))
                listed[head % 2, chunk] = buffer_ref[block, dims.lanes(head)]
            result = lax.dot_general(
                listed[head % 2], weight_refs[head][row], TN, preferred_element_type=jnp.float32
            )
            result = (result * float(HD) ** (-0.5)).astype(jnp.bfloat16)
            for g, part in enumerate(dims.parts(head)):
                out_ref[dims.rows(row), part] = result[:, g * BLK : (g + 1) * BLK].T


def to_head_groups(rows):
    me = lax.axis_index("tp")
    count = lax.axis_size("tp")
    width = rows.shape[1] // count
    parts = []
    for mask in range(count):
        part = lax.dynamic_slice_in_dim(rows, (me ^ mask) * width, width, 1)
        parts.append(part if mask == 0 else swap(part, "tp", mask))
    return jnp.stack(parts)


def to_quarters(pieces):
    me = lax.axis_index("tp")
    count, quarter, width = pieces.shape
    out = jnp.zeros((quarter, count * width), pieces.dtype)
    for mask in range(count):
        part = pieces[mask] if mask == 0 else swap(pieces[mask], "tp", mask)
        out = lax.dynamic_update_slice(out, part, (0, (me ^ mask) * width))
    return out


def cut(*values):
    return lax.optimization_barrier(values)


def held_until(value, *others):
    return lax.optimization_barrier((value, *others))[0]


def with_near(own):
    return swap(own, "ctx", 2), swap(own, "ctx", 4)


def with_diagonal(along_half, across_half):
    return swap(along_half, "ctx", 2), swap(across_half, "ctx", 4)


def to_diagonal(near, got):
    half = near.shape[1] // 2
    to_x = jnp.stack([near[3, :half] + got[3, :half], near[1, :half] + got[1, :half]])
    to_y = jnp.stack([near[3, half:] + got[3, half:], near[2, half:] + got[2, half:]])
    return to_x, to_y


def send_near(near, got, from_x, from_y):
    half = near.shape[1] // 2
    more_b = swap(near[1, half:] + got[1, half:] + from_y[0], "ctx", 2)
    more_a = swap(near[2, :half] + got[2, :half] + from_x[0], "ctx", 4)
    return more_a, more_b


def total_own(near, got, from_x, from_y, more_a, more_b):
    own = near[0] + got[0]
    return own + jnp.concatenate([from_x[1] + more_a, from_y[1] + more_b], axis=0)


def dense_plan(queries, key_rows, value_rows, out_grad, block_list):
    tokens = queries.shape[0]
    blocks = tokens // BLK
    shard_total = lax.axis_size("ctx")
    quarters = lax.axis_size("tp")
    width = block_list.shape[1]
    head_width = key_rows.shape[1] // quarters
    heads = head_width // HD
    group = queries.shape[1] // head_width
    rows = shard_total * tokens
    me_ctx = lax.axis_index("ctx")
    me_tp = lax.axis_index("tp").reshape(1)
    places = ((block_list // blocks) ^ me_ctx) * blocks + block_list % blocks
    places = places.reshape(-1)
    quarter = tokens // quarters
    half = quarters // 2
    pieces = [((shard,), 0, quarters) for shard in (0, 2, 4)]
    pieces += [((6,), 0, half), ((6,), half, half), ((1, 3, 5), 0, quarters)]
    pieces += [((7,), 0, half), ((7,), half, half)]
    dims = Shape(blocks, width, heads, group)
    list_len = width * BLK
    query_rows = group * BLK
    bf16 = jnp.bfloat16

    in_vmem = pl.BlockSpec(memory_space=pltpu.VMEM)
    in_smem = pl.BlockSpec(memory_space=pltpu.SMEM)
    in_hbm = pl.BlockSpec(memory_space=pltpu.HBM)
    queries = pltpu.with_memory_space_constraint(queries, pltpu.HBM)
    out_grad = pltpu.with_memory_space_constraint(out_grad, pltpu.HBM)
    shape = jax.ShapeDtypeStruct
    sums = [shape((shard_total // 2, quarters, quarter, head_width), bf16)] * 2
    stash = shape((blocks, list_len, query_rows), bf16)
    grads = shape((blocks, HD, query_rows), bf16)
    inverses = shape((blocks, 8, query_rows), jnp.float32)
    ordered = shape((rows, head_width), bf16)
    flat = shape(queries.shape, bf16)
    flag = shape((8, HD), jnp.float32)
    one_head = shape((tokens, group * HD), bf16)
    two_rows = pltpu.VMEM((2, list_len, query_rows), jnp.float32)
    total = pltpu.VMEM((rows, head_width), jnp.float32)
    listed = pltpu.VMEM((2, list_len, HD), bf16)
    sem = pltpu.SemaphoreType.DMA

    def call(name, kernel, outs, scratch, scalars, operands):
        return pl.pallas_call(
            kernel,
            in_specs=[in_smem] * len(scalars) + [in_hbm if x is queries or x is out_grad else in_vmem for x in operands],
            out_specs=[in_vmem] * len(outs),
            out_shape=outs,
            scratch_shapes=scratch,
            compiler_params=pltpu.CompilerParams(vmem_limit_bytes=VMEM_MIB * 2**20),
            cost_estimate=pl.CostEstimate(flops=2**32, bytes_accessed=2**20, transcendentals=0),
            name=name,
        )(*scalars, *operands)

    key_own = to_head_groups(key_rows)
    key_x, key_y = with_near(key_own)
    value_own = to_head_groups(value_rows)
    key_x, key_y, key_own, value_own = cut(key_x, key_y, key_own, value_own)
    key_y1, key_x2, key_three = cut(
        key_y[:half], key_x[half:], jnp.concatenate([key_own, key_x, key_y])
    )
    key_d1, key_d2 = with_diagonal(key_y1, key_x2)
    key_d1, key_d2, key_three = cut(key_d1, key_d2, key_three)
    keys = [key_own, key_x, key_y, key_d1, key_d2]
    keys += [swap(part, "ctx", 1) for part in (key_three, key_d1, key_d2)]
    value_x, value_y = with_near(held_until(value_own, key_d1))

    exp_0, grad_0, inverse_0, keys_in_order, query_here, grad_here = call(
        "exps_0", functools.partial(first_exps_kernel, pieces, dims, tokens),
        [stash, grads, inverses, ordered, flat, flat], [two_rows, sem((2 * heads,))],
        (places, me_tp), (queries, out_grad, *keys),
    )
    value_x, value_y, inverse_0 = cut(value_x, value_y, inverse_0)
    value_y1, value_x2, value_three, places_1 = cut(
        value_y[:half], value_x[half:], jnp.concatenate([value_own, value_x, value_y]), places
    )
    value_d1, value_d2 = with_diagonal(value_y1, value_x2)
    value_far = swap(value_three, "ctx", 1)
    exps, grad_ts, inverse = [exp_0], [grad_0], [inverse_0]
    for head in range(1, heads):
        made = call(
            "exps", functools.partial(exps_kernel, head, dims),
            [stash, grads, inverses], [two_rows], (places_1,),
            (query_here, grad_here, keys_in_order),
        )
        for kept, new in zip((exps, grad_ts, inverse), made):
            kept.append(new)
    value_d1, value_d2, value_far, inverse[-1] = cut(value_d1, value_d2, value_far, inverse[-1])
    values = [value_own, value_x, value_y, value_d1, value_d2, value_far]
    values += [swap(part, "ctx", 1) for part in (value_d1, value_d2)]
    value_near, value_away = call(
        "value_sums", functools.partial(values_kernel, dims, tokens),
        sums, [total], (held_until(places, inverse[-1]), me_tp), (*exps, *grad_ts),
    )
    value_near, value_away, places_2, *values[-2:] = cut(value_near, value_away, places, *values[-2:])
    value_got = swap(value_away, "ctx", 1)
    ds, token, attended = [], None, []
    for head in range(heads - 1):
        out, made, values_in_order, token = call(
            "scores", functools.partial(scores_kernel, head, pieces, dims, tokens),
            [one_head, stash, ordered, flag], [listed], (places_2, me_tp),
            (exps[head], grad_ts[head], inverse[head], *values),
        )
        attended.append(out)
        ds.append(made)
    value_got, token = cut(value_got, token)
    to_x, to_y = to_diagonal(value_near, value_got)
    to_x, to_y, places_3 = cut(to_x, to_y, held_until(places, token))
    value_first = swap(to_x, "ctx", 2), swap(to_y, "ctx", 4)
    out, made, key_near, key_away = call(
        "key_sums", functools.partial(keys_kernel, dims, tokens),
        [one_head, stash, *sums], [total, listed], (places_3, me_tp),
        (exps[-1], grad_ts[-1], inverse[-1], values_in_order, *ds, query_here),
    )
    attended.append(out)
    ds.append(made)
    key_near, key_away, places_4, *value_first = cut(key_near, key_away, places, *value_first)
    key_got = swap(key_away, "ctx", 1)
    value_more = send_near(value_near, value_got, *value_first)
    query_grad, token = call(
        "query_grad", functools.partial(rows_kernel, dims),
        [flat, flag], [listed], (places_4,), (keys_in_order, *ds),
    )
    key_got, token = cut(key_got, token)
    to_x, to_y = cut(*to_diagonal(key_near, key_got))
    key_first = swap(to_x, "ctx", 2), swap(to_y, "ctx", 4)
    attended = jnp.concatenate(cut(*attended, to_x, to_y)[:heads], axis=1)
    value_sum = total_own(value_near, value_got, *value_first, *value_more)
    value_grad = to_quarters(held_until(value_sum, attended))
    key_first = cut(*key_first, attended)[:2]
    key_more = send_near(key_near, key_got, *key_first)
    key_sum = total_own(key_near, key_got, *key_first, *key_more)
    return attended, query_grad, to_quarters(key_sum), value_grad


def solution(mesh):
    dense = mesh.shape["ctx"] == DENSE_SHARDS and mesh.shape["tp"] % 4 == 0
    in_specs = (
        P("ctx", "tp"),
        P(("ctx", "tp"), None),
        P(("ctx", "tp"), None),
        P("ctx", "tp"),
        P("ctx", None),
    )
    out_specs = (P("ctx", "tp"), P("ctx", "tp"), P(("ctx", "tp"), None), P(("ctx", "tp"), None))
    return jax.shard_map(
        dense_plan if dense else sparse_plan,
        mesh=mesh,
        in_specs=in_specs,
        out_specs=out_specs,
        check_vma=False,
    )
```

```python
import functools

import jax
import jax.numpy as jnp
from jax import lax
from jax.experimental import pallas as pl
from jax.experimental.pallas import tpu as pltpu
from jax.sharding import PartitionSpec as P

HD = 128
BLK = 128
GLOB = 2
WIN = 3
RAND = 3


def padded_2(cells, sides, width):
    for axis, dim in sides:
        count = lax.axis_size(axis)
        head = lax.slice_in_dim(cells, 0, width, axis=dim)
        tail = lax.slice_in_dim(cells, cells.shape[dim] - width, cells.shape[dim], axis=dim)
        cells = jnp.concatenate(
            [
                lax.ppermute(tail, axis, [(i, (i + 1) % count) for i in range(count)]),
                cells,
                lax.ppermute(head, axis, [((i + 1) % count, i) for i in range(count)]),
            ],
            axis=dim,
        )
    return cells


def spread(x, axis, root):
    mine = lax.axis_index(axis) == root
    return lax.psum(jnp.where(mine, x, jnp.zeros_like(x)), axis)


def shifted(value, axis, steps):
    count = lax.axis_size(axis)
    pairs = [(source, (source + steps) % count) for source in range(count)]
    return lax.ppermute(value, axis, pairs)


def attend_block(tiles):
    query_tile, grad_tile, keys_tile, values_tile = tiles
    inverse_root = float(HD) ** (-0.5)
    scores = (
        jnp.einsum("qkgd,nkd->kgqn", query_tile, keys_tile, preferred_element_type=jnp.float32)
        * inverse_root
    )
    row_max = jnp.max(scores, axis=-1, keepdims=True)
    logsum = row_max + jnp.log(jnp.sum(jnp.exp(scores - row_max), axis=-1, keepdims=True))
    weights_f = jnp.exp(scores - logsum)
    weights_low = weights_f.astype(jnp.bfloat16)
    attended = jnp.einsum(
        "kgqn,nkd->qkgd", weights_low, values_tile, preferred_element_type=jnp.float32
    ).astype(jnp.bfloat16)
    row_delta = jnp.sum(grad_tile.astype(jnp.float32) * attended.astype(jnp.float32), axis=-1)
    row_delta = jnp.transpose(row_delta, (1, 2, 0))
    dweights = jnp.einsum(
        "qkgd,nkd->kgqn", grad_tile, values_tile, preferred_element_type=jnp.float32
    )
    dscores_low = (weights_f * (dweights - row_delta[..., None])).astype(jnp.bfloat16)
    query_grad = (
        jnp.einsum("kgqn,nkd->qkgd", dscores_low, keys_tile, preferred_element_type=jnp.float32)
        * inverse_root
    ).astype(jnp.bfloat16)
    value_part = jnp.einsum(
        "kgqn,qkgd->nkd", weights_low, grad_tile, preferred_element_type=jnp.float32
    )
    key_part = (
        jnp.einsum("kgqn,qkgd->nkd", dscores_low, query_tile, preferred_element_type=jnp.float32)
        * inverse_root
    )
    return (attended, query_grad, key_part, value_part)


def sparse_plan(queries, key_rows, value_rows, out_grad, block_list):
    tokens_here = queries.shape[0]
    block_count = tokens_here // BLK
    shard_total = lax.axis_size("ctx")
    my_index = lax.axis_index("ctx")
    local_keys, local_values = (
        lax.all_to_all(key_rows, "tp", split_axis=1, concat_axis=0, tiled=True),
        lax.all_to_all(value_rows, "tp", split_axis=1, concat_axis=0, tiled=True),
    )
    head_width = local_keys.shape[1]
    kv_heads = head_width // HD
    both_width = 2 * head_width
    joined = jnp.concatenate([local_keys, local_values], axis=1)
    joined_blocks = joined.reshape(block_count, BLK, both_width)
    padded = padded_2(joined, (("ctx", 0),), BLK)
    padded = padded.reshape(block_count + 2, BLK, both_width)
    window_kv = jnp.stack(
        [padded[0:block_count], padded[1 : block_count + 1], padded[2 : block_count + 2]], axis=1
    )
    global_ids = block_list[0, 0:GLOB]
    global_owner = global_ids // block_count
    global_local = global_ids % block_count
    fetched_list = []
    for column in range(GLOB):
        owned = lax.dynamic_index_in_dim(joined_blocks, global_local[column], 0, keepdims=False)
        fetched_list.append(spread(owned, "ctx", global_owner[column]))
    global_kv = jnp.stack(fetched_list, axis=0)
    random_ids = block_list[:, GLOB + WIN :].reshape(-1)
    ref_count = random_ids.shape[0]
    capacity = (ref_count + shard_total - 1) // shard_total
    slot_count = shard_total * capacity
    ref_owner = random_ids // block_count
    ref_local = random_ids % block_count
    ref_order = jnp.arange(ref_count, dtype=jnp.int32)
    earlier = (ref_owner[:, None] == ref_owner[None, :]) & (ref_order[None, :] < ref_order[:, None])
    ref_rank = jnp.sum(earlier, axis=1)
    ref_slot = ref_owner * capacity + ref_rank
    slot_hit = ref_slot[:, None] == jnp.arange(slot_count, dtype=jnp.int32)[None, :]
    wanted = jnp.sum(jnp.where(slot_hit, ref_local[:, None] + 1, 0), axis=0) - 1
    asked = lax.all_to_all(
        wanted.reshape(shard_total, capacity), "ctx", split_axis=0, concat_axis=0, tiled=True
    )
    valid_ask = asked >= 0
    served = jnp.where(
        valid_ask[:, :, None, None],
        joined_blocks[jnp.maximum(asked, 0)],
        jnp.zeros((), jnp.bfloat16),
    )
    arrived = lax.all_to_all(served, "ctx", split_axis=0, concat_axis=0, tiled=True).reshape(
        slot_count, BLK, both_width
    )
    random_kv = arrived[ref_slot].reshape(block_count, RAND, BLK, both_width)
    list_len = GLOB + WIN + RAND
    global_rep = jnp.broadcast_to(global_kv[None], (block_count, GLOB, BLK, both_width))
    listed_kv = jnp.concatenate([global_rep, window_kv, random_kv], axis=1)
    keys_here = listed_kv[..., :head_width].reshape(block_count, list_len * BLK, kv_heads, HD)
    values_here = listed_kv[..., head_width:].reshape(block_count, list_len * BLK, kv_heads, HD)
    group_size = queries.shape[1] // head_width
    query_tiles = queries.reshape(block_count, BLK, kv_heads, group_size, HD)
    grad_tiles = out_grad.reshape(block_count, BLK, kv_heads, group_size, HD)
    attended, query_grad, key_part, value_part = lax.map(
        attend_block, (query_tiles, grad_tiles, keys_here, values_here)
    )
    grad_kv = jnp.concatenate(
        [
            key_part.reshape(block_count, list_len, BLK, head_width),
            value_part.reshape(block_count, list_len, BLK, head_width),
        ],
        axis=-1,
    )
    window_grad = grad_kv[:, GLOB : GLOB + WIN]
    zero_block = jnp.zeros((1, BLK, both_width), jnp.float32)
    rim_acc = (
        jnp.concatenate([window_grad[:, 0], zero_block, zero_block], axis=0)
        + jnp.concatenate([zero_block, window_grad[:, 1], zero_block], axis=0)
        + jnp.concatenate([zero_block, zero_block, window_grad[:, 2]], axis=0)
    )
    from_left = shifted(rim_acc[block_count + 1].astype(jnp.bfloat16), "ctx", 1).astype(jnp.float32)
    from_right = shifted(rim_acc[0].astype(jnp.bfloat16), "ctx", -1).astype(jnp.float32)
    own_grads = rim_acc[1 : block_count + 1]
    own_grads = own_grads.at[0].add(from_left)
    own_grads = own_grads.at[block_count - 1].add(from_right)
    global_terms = lax.psum(jnp.sum(grad_kv[:, 0:GLOB], axis=0), "ctx")
    global_place = (global_local[:, None] == jnp.arange(block_count, dtype=jnp.int32)[None, :]) & (
        global_owner == my_index
    )[:, None]
    own_grads = own_grads + jnp.einsum(
        "ro,rhn->ohn",
        global_place.astype(jnp.float32),
        global_terms,
        precision=lax.Precision.HIGHEST,
    )
    random_grad = grad_kv[:, GLOB + WIN :].reshape(ref_count, BLK, both_width)
    outgoing = jnp.zeros((slot_count, BLK, both_width), jnp.float32).at[ref_slot].set(random_grad)
    returned = lax.all_to_all(
        outgoing.reshape(shard_total, capacity, BLK, both_width).astype(jnp.bfloat16),
        "ctx",
        split_axis=0,
        concat_axis=0,
        tiled=True,
    ).astype(jnp.float32)
    returned = returned.reshape(slot_count, BLK, both_width)
    slot_place = (
        asked.reshape(slot_count)[:, None] == jnp.arange(block_count, dtype=jnp.int32)[None, :]
    ).astype(jnp.float32)
    own_grads = own_grads + jnp.einsum(
        "sj,sxc->jxc", slot_place, returned, precision=lax.Precision.HIGHEST
    )
    own_grads = own_grads.reshape(tokens_here, both_width).astype(jnp.bfloat16)
    key_grad, value_grad = (
        lax.all_to_all(own_grads[:, :head_width], "tp", split_axis=0, concat_axis=1, tiled=True),
        lax.all_to_all(own_grads[:, head_width:], "tp", split_axis=0, concat_axis=1, tiled=True),
    )
    return (
        attended.reshape(tokens_here, -1),
        query_grad.reshape(tokens_here, -1),
        key_grad,
        value_grad,
    )


LOG2E = 1.4426950408889634
DENSE_SHARDS = 8
VMEM_MIB = 8
NT = (((1,), (1,)), ((), ()))
TN = (((0,), (0,)), ((), ()))


def swap(value, axis, mask):
    count = lax.axis_size(axis)
    return lax.ppermute(value, axis, [(i, i ^ mask) for i in range(count)])


def rows_of(quarter, shard, spot, tokens, me_tp):
    return pl.ds(pl.multiple_of(shard * tokens + (spot ^ me_tp) * quarter, 16), quarter)


def place_pieces(piece_refs, pieces, tokens, me_tp, buffer):
    for ref, (shards, first, spots) in zip(piece_refs, pieces):
        for at in range(ref.shape[0]):
            shard, spot = shards[at // spots], first + at % spots
            buffer[rows_of(ref.shape[1], shard, spot, tokens, me_tp)] = ref[at]


def write_sums(accs, out_refs, tokens, me_tp, scale):
    near_ref, far_ref = out_refs
    for k in range(near_ref.shape[0]):
        for ref, shard in ((far_ref.at[k], 2 * k + 1), (near_ref.at[k], 2 * k)):
            for spot in range(ref.shape[0]):
                rows = rows_of(ref.shape[1], shard, spot, tokens, me_tp)
                for at, acc in enumerate(accs):
                    part = acc[rows]
                    if scale is not None:
                        part = part * scale
                    lanes = slice(at * part.shape[1], (at + 1) * part.shape[1])
                    ref[spot, :, lanes] = part.astype(ref.dtype)


def block_of(place_ref, entry):
    return pl.ds(pl.multiple_of(place_ref[entry] * BLK, BLK), BLK)


def fold(value, op):
    rows, width = value.shape
    return op(value.reshape(rows // 8, 8, width), axis=0)


def joined(op, total, value):
    return value if total is None else op(total, value)


class Shape:
    def __init__(self, blocks, width, heads, group):
        self.blocks, self.width, self.heads, self.group = blocks, width, heads, group

    def rows(self, row):
        return slice(row * BLK, (row + 1) * BLK)

    def lanes(self, head):
        return slice(head * HD, (head + 1) * HD)

    def parts(self, head):
        first = head * self.group
        return [slice((first + g) * HD, (first + g + 1) * HD) for g in range(self.group)]

    def wide(self, head):
        return slice(head * self.group * HD, (head + 1) * self.group * HD)

    def chunks(self):
        return [(c, slice(c * BLK, (c + 1) * BLK)) for c in range(self.width)]

    def entry(self, row, column):
        return row * self.width + column

    def stacked(self, ref, row, head):
        return jnp.concatenate([ref[self.rows(row), part] for part in self.parts(head)], axis=0)

    def flipped(self, ref, row, head):
        return jnp.concatenate([ref[self.rows(row), part].T for part in self.parts(head)], axis=1)


def first_exps_kernel(pieces, dims, tokens, place_ref, tp_ref, query_hbm, grad_hbm, *refs):
    count = len(pieces)
    exp_ref, grad_t_ref, inv_ref, acc, buffer, query, grad, score_ref, sems = refs[count:]
    copies = []
    for head in range(dims.heads):
        for source, target in ((query_hbm, query), (grad_hbm, grad)):
            lanes = dims.wide(head)
            copies.append(
                pltpu.make_async_copy(source.at[:, lanes], target.at[:, lanes], sems.at[len(copies)])
            )
            copies[-1].start()
    place_pieces(refs[:count], pieces, tokens, tp_ref[0], buffer)
    copies[0].wait()
    copies[1].wait()
    exp_rows(0, dims, place_ref, query, grad, buffer, exp_ref, grad_t_ref, inv_ref, score_ref)
    add_values(acc, dims, place_ref, exp_ref, grad_t_ref)
    for copy in copies[2:]:
        copy.wait()


def exps_kernel(head, dims, tokens, place_ref, tp_ref, query, grad, buffer, *refs):
    accs, refs = refs[:head], refs[head:]
    exp_ref, grad_t_ref, inv_ref, *sum_refs, acc, score_ref = refs
    exp_rows(head, dims, place_ref, query, grad, buffer, exp_ref, grad_t_ref, inv_ref, score_ref)
    add_values(acc, dims, place_ref, exp_ref, grad_t_ref)
    write_sums([*accs, acc], sum_refs, tokens, tp_ref[0], None)


def exp_rows(head, dims, place_ref, query, grad, buffer, exp_ref, grad_t_ref, inv_ref, score_ref):
    factor = LOG2E * float(HD) ** (-0.5)
    lanes = dims.lanes(head)
    tops = {}
    for step in range(dims.blocks + 1):
        first, second = step, step - 1
        top_new = total = None
        if first < dims.blocks:
            stacked = dims.stacked(query, first, head)
        if 0 <= second:
            top = jnp.max(tops[second], axis=0, keepdims=True) * factor
        for column, chunk in dims.chunks():
            if first < dims.blocks:
                keys = buffer[block_of(place_ref, dims.entry(first, column)), lanes]
                score = lax.dot_general(keys, stacked, NT, preferred_element_type=jnp.float32)
                score_ref[first % 2, chunk] = score
                top_new = joined(jnp.maximum, top_new, fold(score, jnp.max))
            if 0 <= second:
                weight = jnp.exp2(score_ref[second % 2, chunk] * factor - top)
                exp_ref[second, chunk] = weight.astype(jnp.bfloat16)
                total = joined(jnp.add, total, fold(weight, jnp.sum))
        tops[first] = top_new
        if 0 <= second:
            inverse = 1.0 / jnp.sum(total, axis=0, keepdims=True)
            inv_ref[second] = jnp.broadcast_to(inverse, inv_ref.shape[1:])
            grad_t = dims.flipped(grad, second, head).astype(jnp.float32)
            grad_t_ref[second] = (grad_t * inverse).astype(jnp.bfloat16)


def add_values(acc, dims, place_ref, exp_ref, grad_t_ref):
    acc[...] = jnp.zeros_like(acc)
    for row in range(dims.blocks):
        for column, chunk in dims.chunks():
            acc[block_of(place_ref, dims.entry(row, column))] += lax.dot_general(
                exp_ref[row, chunk], grad_t_ref[row], NT, preferred_element_type=jnp.float32
            )


def add_keys(acc, dims, place_ref, row, head, ds_ref, query):
    stacked = dims.stacked(query, row, head)
    for column, chunk in dims.chunks():
        acc[block_of(place_ref, dims.entry(row, column)), dims.lanes(head)] += jnp.dot(
            ds_ref[row, chunk], stacked, preferred_element_type=jnp.float32
        )


def score_rows(head, dims, place_ref, exp_ref, grad_t_ref, inv_ref, buffer, out_ref, ds_ref, listed, then):
    lanes = dims.lanes(head)
    for row in range(dims.blocks):
        slot = row % 2
        for column, chunk in dims.chunks():
            listed[slot, chunk] = buffer[block_of(place_ref, dims.entry(row, column)), lanes]
        attended = lax.dot_general(
            listed[slot], exp_ref[row], TN, preferred_element_type=jnp.float32
        )
        attended = (attended * inv_ref[row, 0:1]).astype(jnp.bfloat16)
        grad_t = grad_t_ref[row]
        delta = jnp.sum(
            grad_t.astype(jnp.float32) * attended.astype(jnp.float32), axis=0, keepdims=True
        )
        for g, part in enumerate(dims.parts(0)):
            out_ref[dims.rows(row), part] = attended[:, g * BLK : (g + 1) * BLK].T
        for column, chunk in dims.chunks():
            dprob = jnp.dot(listed[slot, chunk], grad_t, preferred_element_type=jnp.float32)
            weight = exp_ref[row, chunk].astype(jnp.float32)
            ds_ref[row, chunk] = (weight * (dprob - delta)).astype(jnp.bfloat16)
        then(row)


def scores_kernel(head, pieces, dims, tokens, place_ref, tp_ref, exp_ref, grad_t_ref, inv_ref, *refs):
    count = len(pieces)
    out_ref, ds_ref, buffer, flag_ref, listed = refs[count:]
    flag_ref[...] = jnp.zeros_like(flag_ref)
    place_pieces(refs[:count], pieces, tokens, tp_ref[0], buffer)
    score_rows(
        head, dims, place_ref, exp_ref, grad_t_ref, inv_ref, buffer, out_ref, ds_ref, listed,
        lambda row: None,
    )


def keys_kernel(dims, tokens, place_ref, tp_ref, exp_ref, grad_t_ref, inv_ref, buffer, *refs):
    done_refs, query = refs[: dims.heads - 1], refs[dims.heads - 1]
    out_ref, ds_ref, *sum_refs, acc, listed = refs[dims.heads :]
    acc[...] = jnp.zeros_like(acc)

    def then(row):
        for head, done_ref in enumerate(done_refs):
            add_keys(acc, dims, place_ref, row, head, done_ref, query)
        add_keys(acc, dims, place_ref, row, dims.heads - 1, ds_ref, query)

    score_rows(
        dims.heads - 1, dims, place_ref, exp_ref, grad_t_ref, inv_ref, buffer, out_ref, ds_ref,
        listed, then,
    )
    write_sums([acc], sum_refs, tokens, tp_ref[0], float(HD) ** (-0.5))


def rows_kernel(dims, place_ref, buffer_ref, *refs):
    weight_refs = refs[: dims.heads]
    out_ref, flag_ref, listed = refs[dims.heads :]
    flag_ref[...] = jnp.zeros_like(flag_ref)
    for row in range(dims.blocks):
        for head in range(dims.heads):
            for column, chunk in dims.chunks():
                block = block_of(place_ref, dims.entry(row, column))
                listed[head % 2, chunk] = buffer_ref[block, dims.lanes(head)]
            result = lax.dot_general(
                listed[head % 2], weight_refs[head][row], TN, preferred_element_type=jnp.float32
            )
            result = (result * float(HD) ** (-0.5)).astype(jnp.bfloat16)
            for g, part in enumerate(dims.parts(head)):
                out_ref[dims.rows(row), part] = result[:, g * BLK : (g + 1) * BLK].T


def to_head_groups(rows):
    me = lax.axis_index("tp")
    count = lax.axis_size("tp")
    width = rows.shape[1] // count
    parts = {}
    for mask in reversed(range(count)):
        part = lax.dynamic_slice_in_dim(rows, (me ^ mask) * width, width, 1)
        parts[mask] = part if mask == 0 else swap(part, "tp", mask)
    return jnp.stack([parts[mask] for mask in range(count)])


def to_quarters(pieces):
    me = lax.axis_index("tp")
    count, quarter, width = pieces.shape
    out = jnp.zeros((quarter, count * width), pieces.dtype)
    for mask in range(count):
        part = pieces[mask] if mask == 0 else swap(pieces[mask], "tp", mask)
        out = lax.dynamic_update_slice(out, part, (0, (me ^ mask) * width))
    return out


def cut(*values):
    return lax.optimization_barrier(values)


def held_until(value, *others):
    return lax.optimization_barrier((value, *others))[0]


def with_near(own):
    return swap(own, "ctx", 2), swap(own, "ctx", 4)


def swap_diagonal(value):
    count = lax.axis_size("ctx")
    return lax.ppermute(value, "ctx", [(i, i ^ (4 if i % 2 else 2)) for i in range(count)])


def pick(first, second):
    odd = lax.axis_index("ctx") % 2 == 1
    return jnp.where(odd, second, first)


def to_neighbours(near, got, diagonal):
    nothing = jnp.zeros_like(diagonal)
    to_x = near[1] + got[1] + pick(nothing, diagonal)
    to_y = near[2] + got[2] + pick(diagonal, nothing)
    return to_x, to_y


def total_own(near, got, from_x, from_y):
    return near[0] + got[0] + from_x + from_y


def dense_plan(queries, key_rows, value_rows, out_grad, block_list):
    tokens = queries.shape[0]
    blocks = tokens // BLK
    shard_total = lax.axis_size("ctx")
    quarters = lax.axis_size("tp")
    width = block_list.shape[1]
    head_width = key_rows.shape[1] // quarters
    heads = head_width // HD
    group = queries.shape[1] // head_width
    rows = shard_total * tokens
    me_ctx = lax.axis_index("ctx")
    me_tp = lax.axis_index("tp").reshape(1)
    places = ((block_list // blocks) ^ me_ctx) * blocks + block_list % blocks
    places = places.reshape(-1)
    quarter = tokens // quarters
    pieces = [((shard,), 0, quarters) for shard in (0, 2, 4, 6)]
    pieces += [((1, 3, 5), 0, quarters), ((7,), 0, quarters)]
    dims = Shape(blocks, width, heads, group)
    list_len = width * BLK
    query_rows = group * BLK
    bf16 = jnp.bfloat16

    in_vmem = pl.BlockSpec(memory_space=pltpu.VMEM)
    in_smem = pl.BlockSpec(memory_space=pltpu.SMEM)
    in_hbm = pl.BlockSpec(memory_space=pltpu.HBM)
    queries = pltpu.with_memory_space_constraint(queries, pltpu.HBM)
    out_grad = pltpu.with_memory_space_constraint(out_grad, pltpu.HBM)
    shape = jax.ShapeDtypeStruct
    sums = [shape((shard_total // 2, quarters, quarter, head_width), bf16)] * 2
    stash = shape((blocks, list_len, query_rows), bf16)
    grads = shape((blocks, HD, query_rows), bf16)
    inverses = shape((blocks, 8, query_rows), jnp.float32)
    ordered = shape((rows, head_width), bf16)
    flat = shape(queries.shape, bf16)
    flag = shape((8, HD), jnp.float32)
    one_head = shape((tokens, group * HD), bf16)
    two_rows = pltpu.VMEM((2, list_len, query_rows), jnp.float32)
    total = pltpu.VMEM((rows, head_width), jnp.float32)
    head_sum = shape((rows, HD), jnp.float32)
    head_total = pltpu.VMEM((rows, HD), jnp.float32)
    listed = pltpu.VMEM((2, list_len, HD), bf16)
    sem = pltpu.SemaphoreType.DMA

    def call(name, kernel, outs, scratch, scalars, operands):
        return pl.pallas_call(
            kernel,
            in_specs=[in_smem] * len(scalars) + [in_hbm if x is queries or x is out_grad else in_vmem for x in operands],
            out_specs=[in_vmem] * len(outs),
            out_shape=outs,
            scratch_shapes=scratch,
            compiler_params=pltpu.CompilerParams(vmem_limit_bytes=VMEM_MIB * 2**20),
            cost_estimate=pl.CostEstimate(flops=2**32, bytes_accessed=2**20, transcendentals=0),
            name=name,
        )(*scalars, *operands)

    key_own = to_head_groups(key_rows)
    key_x, key_y = with_near(key_own)
    value_own = to_head_groups(value_rows)
    key_x, key_y, key_own, value_own = cut(key_x, key_y, key_own, value_own)
    key_next, key_three = cut(pick(key_y, key_x), jnp.concatenate([key_own, key_x, key_y]))
    key_diag, key_three = cut(swap_diagonal(key_next), key_three)
    keys = [key_own, key_x, key_y, key_diag]
    keys += [swap(part, "ctx", 1) for part in (key_three, key_diag)]
    value_x, value_y = with_near(held_until(value_own, key_diag))

    exp_0, grad_0, inverse_0, sum_0, keys_in_order, query_here, grad_here = call(
        "exps_0", functools.partial(first_exps_kernel, pieces, dims, tokens),
        [stash, grads, inverses, head_sum, ordered, flat, flat], [two_rows, sem((2 * heads,))],
        (places, me_tp), (queries, out_grad, *keys),
    )
    value_x, value_y, inverse_0 = cut(value_x, value_y, inverse_0)
    value_next, value_three, places_1 = cut(
        pick(value_y, value_x), jnp.concatenate([value_own, value_x, value_y]), places
    )
    value_diag = swap_diagonal(value_next)
    value_far = swap(value_three, "ctx", 1)
    exp_1, grad_1, inverse_1, value_near, value_away = call(
        "exps", functools.partial(exps_kernel, 1, dims, tokens),
        [stash, grads, inverses, *sums], [head_total, two_rows], (places_1, me_tp),
        (query_here, grad_here, keys_in_order, sum_0),
    )
    exps, grad_ts, inverse = (exp_0, exp_1), (grad_0, grad_1), (inverse_0, inverse_1)
    value_diag, value_far, value_near, value_away = cut(
        value_diag, value_far, value_near, value_away
    )
    value_last = swap(value_diag, "ctx", 1)
    value_away, places_2, value_last = cut(value_away, places, value_last)
    values = [value_own, value_x, value_y, value_diag, value_far, value_last]
    value_got = swap(value_away, "ctx", 1)
    ds, token, attended = [], None, []
    for head in range(heads - 1):
        out, made, values_in_order, token = call(
            "scores", functools.partial(scores_kernel, head, pieces, dims, tokens),
            [one_head, stash, ordered, flag], [listed], (places_2, me_tp),
            (exps[head], grad_ts[head], inverse[head], *values),
        )
        attended.append(out)
        ds.append(made)
    value_got, token = cut(value_got, token)
    diagonal, places_3 = cut(value_near[3] + value_got[3], held_until(places, token))
    value_first = swap_diagonal(diagonal)
    out, made, key_near, key_away = call(
        "key_sums", functools.partial(keys_kernel, dims, tokens),
        [one_head, stash, *sums], [total, listed], (places_3, me_tp),
        (exps[-1], grad_ts[-1], inverse[-1], values_in_order, *ds, query_here),
    )
    attended.append(out)
    ds.append(made)
    key_near, key_away, places_4, value_first = cut(key_near, key_away, places, value_first)
    key_got = swap(key_away, "ctx", 1)
    to_x, to_y = to_neighbours(value_near, value_got, value_first)
    value_more = swap(to_x, "ctx", 2), swap(to_y, "ctx", 4)
    query_grad, token = call(
        "query_grad", functools.partial(rows_kernel, dims),
        [flat, flag], [listed], (places_4,), (keys_in_order, *ds),
    )
    key_got, token = cut(key_got, token)
    diagonal = held_until(key_near[3] + key_got[3], token)
    key_first = swap_diagonal(diagonal)
    attended = jnp.concatenate(cut(*attended, diagonal)[:heads], axis=1)
    attended, *value_more = cut(attended, *value_more)
    value_sum = total_own(value_near, value_got, *value_more)
    key_first, attended = cut(key_first, attended)
    to_x, to_y = to_neighbours(key_near, key_got, key_first)
    value_grad = to_quarters(value_sum)
    key_more = swap(to_x, "ctx", 2), swap(to_y, "ctx", 4)
    key_sum = total_own(key_near, key_got, *key_more)
    return attended, query_grad, to_quarters(key_sum), value_grad


def solution(mesh):
    dense = mesh.shape["ctx"] == DENSE_SHARDS and mesh.shape["tp"] % 4 == 0
    in_specs = (
        P("ctx", "tp"),
        P(("ctx", "tp"), None),
        P(("ctx", "tp"), None),
        P("ctx", "tp"),
        P("ctx", None),
    )
    out_specs = (P("ctx", "tp"), P("ctx", "tp"), P(("ctx", "tp"), None), P(("ctx", "tp"), None))
    return jax.shard_map(
        dense_plan if dense else sparse_plan,
        mesh=mesh,
        in_specs=in_specs,
        out_specs=out_specs,
        check_vma=False,
    )
```

```python
import functools

import jax
import jax.numpy as jnp
from jax import lax
from jax.experimental import pallas as pl
from jax.experimental.pallas import tpu as pltpu
from jax.sharding import PartitionSpec as P

HD = 128
BLK = 128
GLOB = 2
WIN = 3
RAND = 3


def padded_2(cells, sides, width):
    for axis, dim in sides:
        count = lax.axis_size(axis)
        head = lax.slice_in_dim(cells, 0, width, axis=dim)
        tail = lax.slice_in_dim(cells, cells.shape[dim] - width, cells.shape[dim], axis=dim)
        cells = jnp.concatenate(
            [
                lax.ppermute(tail, axis, [(i, (i + 1) % count) for i in range(count)]),
                cells,
                lax.ppermute(head, axis, [((i + 1) % count, i) for i in range(count)]),
            ],
            axis=dim,
        )
    return cells


def spread(x, axis, root):
    mine = lax.axis_index(axis) == root
    return lax.psum(jnp.where(mine, x, jnp.zeros_like(x)), axis)


def shifted(value, axis, steps):
    count = lax.axis_size(axis)
    pairs = [(source, (source + steps) % count) for source in range(count)]
    return lax.ppermute(value, axis, pairs)


def attend_block(tiles):
    query_tile, grad_tile, keys_tile, values_tile = tiles
    inverse_root = float(HD) ** (-0.5)
    scores = (
        jnp.einsum("qkgd,nkd->kgqn", query_tile, keys_tile, preferred_element_type=jnp.float32)
        * inverse_root
    )
    row_max = jnp.max(scores, axis=-1, keepdims=True)
    logsum = row_max + jnp.log(jnp.sum(jnp.exp(scores - row_max), axis=-1, keepdims=True))
    weights_f = jnp.exp(scores - logsum)
    weights_low = weights_f.astype(jnp.bfloat16)
    attended = jnp.einsum(
        "kgqn,nkd->qkgd", weights_low, values_tile, preferred_element_type=jnp.float32
    ).astype(jnp.bfloat16)
    row_delta = jnp.sum(grad_tile.astype(jnp.float32) * attended.astype(jnp.float32), axis=-1)
    row_delta = jnp.transpose(row_delta, (1, 2, 0))
    dweights = jnp.einsum(
        "qkgd,nkd->kgqn", grad_tile, values_tile, preferred_element_type=jnp.float32
    )
    dscores_low = (weights_f * (dweights - row_delta[..., None])).astype(jnp.bfloat16)
    query_grad = (
        jnp.einsum("kgqn,nkd->qkgd", dscores_low, keys_tile, preferred_element_type=jnp.float32)
        * inverse_root
    ).astype(jnp.bfloat16)
    value_part = jnp.einsum(
        "kgqn,qkgd->nkd", weights_low, grad_tile, preferred_element_type=jnp.float32
    )
    key_part = (
        jnp.einsum("kgqn,qkgd->nkd", dscores_low, query_tile, preferred_element_type=jnp.float32)
        * inverse_root
    )
    return (attended, query_grad, key_part, value_part)


def sparse_plan(queries, key_rows, value_rows, out_grad, block_list):
    tokens_here = queries.shape[0]
    block_count = tokens_here // BLK
    shard_total = lax.axis_size("ctx")
    my_index = lax.axis_index("ctx")
    local_keys, local_values = (
        lax.all_to_all(key_rows, "tp", split_axis=1, concat_axis=0, tiled=True),
        lax.all_to_all(value_rows, "tp", split_axis=1, concat_axis=0, tiled=True),
    )
    head_width = local_keys.shape[1]
    kv_heads = head_width // HD
    both_width = 2 * head_width
    joined = jnp.concatenate([local_keys, local_values], axis=1)
    joined_blocks = joined.reshape(block_count, BLK, both_width)
    padded = padded_2(joined, (("ctx", 0),), BLK)
    padded = padded.reshape(block_count + 2, BLK, both_width)
    window_kv = jnp.stack(
        [padded[0:block_count], padded[1 : block_count + 1], padded[2 : block_count + 2]], axis=1
    )
    global_ids = block_list[0, 0:GLOB]
    global_owner = global_ids // block_count
    global_local = global_ids % block_count
    fetched_list = []
    for column in range(GLOB):
        owned = lax.dynamic_index_in_dim(joined_blocks, global_local[column], 0, keepdims=False)
        fetched_list.append(spread(owned, "ctx", global_owner[column]))
    global_kv = jnp.stack(fetched_list, axis=0)
    random_ids = block_list[:, GLOB + WIN :].reshape(-1)
    ref_count = random_ids.shape[0]
    capacity = (ref_count + shard_total - 1) // shard_total
    slot_count = shard_total * capacity
    ref_owner = random_ids // block_count
    ref_local = random_ids % block_count
    ref_order = jnp.arange(ref_count, dtype=jnp.int32)
    earlier = (ref_owner[:, None] == ref_owner[None, :]) & (ref_order[None, :] < ref_order[:, None])
    ref_rank = jnp.sum(earlier, axis=1)
    ref_slot = ref_owner * capacity + ref_rank
    slot_hit = ref_slot[:, None] == jnp.arange(slot_count, dtype=jnp.int32)[None, :]
    wanted = jnp.sum(jnp.where(slot_hit, ref_local[:, None] + 1, 0), axis=0) - 1
    asked = lax.all_to_all(
        wanted.reshape(shard_total, capacity), "ctx", split_axis=0, concat_axis=0, tiled=True
    )
    valid_ask = asked >= 0
    served = jnp.where(
        valid_ask[:, :, None, None],
        joined_blocks[jnp.maximum(asked, 0)],
        jnp.zeros((), jnp.bfloat16),
    )
    arrived = lax.all_to_all(served, "ctx", split_axis=0, concat_axis=0, tiled=True).reshape(
        slot_count, BLK, both_width
    )
    random_kv = arrived[ref_slot].reshape(block_count, RAND, BLK, both_width)
    list_len = GLOB + WIN + RAND
    global_rep = jnp.broadcast_to(global_kv[None], (block_count, GLOB, BLK, both_width))
    listed_kv = jnp.concatenate([global_rep, window_kv, random_kv], axis=1)
    keys_here = listed_kv[..., :head_width].reshape(block_count, list_len * BLK, kv_heads, HD)
    values_here = listed_kv[..., head_width:].reshape(block_count, list_len * BLK, kv_heads, HD)
    group_size = queries.shape[1] // head_width
    query_tiles = queries.reshape(block_count, BLK, kv_heads, group_size, HD)
    grad_tiles = out_grad.reshape(block_count, BLK, kv_heads, group_size, HD)
    attended, query_grad, key_part, value_part = lax.map(
        attend_block, (query_tiles, grad_tiles, keys_here, values_here)
    )
    grad_kv = jnp.concatenate(
        [
            key_part.reshape(block_count, list_len, BLK, head_width),
            value_part.reshape(block_count, list_len, BLK, head_width),
        ],
        axis=-1,
    )
    window_grad = grad_kv[:, GLOB : GLOB + WIN]
    zero_block = jnp.zeros((1, BLK, both_width), jnp.float32)
    rim_acc = (
        jnp.concatenate([window_grad[:, 0], zero_block, zero_block], axis=0)
        + jnp.concatenate([zero_block, window_grad[:, 1], zero_block], axis=0)
        + jnp.concatenate([zero_block, zero_block, window_grad[:, 2]], axis=0)
    )
    from_left = shifted(rim_acc[block_count + 1].astype(jnp.bfloat16), "ctx", 1).astype(jnp.float32)
    from_right = shifted(rim_acc[0].astype(jnp.bfloat16), "ctx", -1).astype(jnp.float32)
    own_grads = rim_acc[1 : block_count + 1]
    own_grads = own_grads.at[0].add(from_left)
    own_grads = own_grads.at[block_count - 1].add(from_right)
    global_terms = lax.psum(jnp.sum(grad_kv[:, 0:GLOB], axis=0), "ctx")
    global_place = (global_local[:, None] == jnp.arange(block_count, dtype=jnp.int32)[None, :]) & (
        global_owner == my_index
    )[:, None]
    own_grads = own_grads + jnp.einsum(
        "ro,rhn->ohn",
        global_place.astype(jnp.float32),
        global_terms,
        precision=lax.Precision.HIGHEST,
    )
    random_grad = grad_kv[:, GLOB + WIN :].reshape(ref_count, BLK, both_width)
    outgoing = jnp.zeros((slot_count, BLK, both_width), jnp.float32).at[ref_slot].set(random_grad)
    returned = lax.all_to_all(
        outgoing.reshape(shard_total, capacity, BLK, both_width).astype(jnp.bfloat16),
        "ctx",
        split_axis=0,
        concat_axis=0,
        tiled=True,
    ).astype(jnp.float32)
    returned = returned.reshape(slot_count, BLK, both_width)
    slot_place = (
        asked.reshape(slot_count)[:, None] == jnp.arange(block_count, dtype=jnp.int32)[None, :]
    ).astype(jnp.float32)
    own_grads = own_grads + jnp.einsum(
        "sj,sxc->jxc", slot_place, returned, precision=lax.Precision.HIGHEST
    )
    own_grads = own_grads.reshape(tokens_here, both_width).astype(jnp.bfloat16)
    key_grad, value_grad = (
        lax.all_to_all(own_grads[:, :head_width], "tp", split_axis=0, concat_axis=1, tiled=True),
        lax.all_to_all(own_grads[:, head_width:], "tp", split_axis=0, concat_axis=1, tiled=True),
    )
    return (
        attended.reshape(tokens_here, -1),
        query_grad.reshape(tokens_here, -1),
        key_grad,
        value_grad,
    )


LOG2E = 1.4426950408889634
DENSE_SHARDS = 8
VMEM_MIB = 8
NT = (((1,), (1,)), ((), ()))
TN = (((0,), (0,)), ((), ()))


def swap(value, axis, mask):
    count = lax.axis_size(axis)
    return lax.ppermute(value, axis, [(i, i ^ mask) for i in range(count)])


def rows_of(quarter, shard, spot, tokens, me_tp):
    return pl.ds(pl.multiple_of(shard * tokens + (spot ^ me_tp) * quarter, 16), quarter)


def place_pieces(piece_refs, pieces, tokens, me_tp, buffer):
    for ref, (shards, first, spots) in zip(piece_refs, pieces):
        for at in range(ref.shape[0]):
            shard, spot = shards[at // spots], first + at % spots
            buffer[rows_of(ref.shape[1], shard, spot, tokens, me_tp)] = ref[at]


def write_sums(accs, out_refs, tokens, me_tp, scale):
    near_ref, far_ref = out_refs
    for k in range(near_ref.shape[0]):
        for ref, shard in ((far_ref.at[k], 2 * k + 1), (near_ref.at[k], 2 * k)):
            for spot in range(ref.shape[0]):
                rows = rows_of(ref.shape[1], shard, spot, tokens, me_tp)
                for at, acc in enumerate(accs):
                    part = acc[rows]
                    if scale is not None:
                        part = part * scale
                    lanes = slice(at * part.shape[1], (at + 1) * part.shape[1])
                    ref[spot, :, lanes] = part.astype(ref.dtype)


def block_of(place_ref, entry):
    return pl.ds(pl.multiple_of(place_ref[entry] * BLK, BLK), BLK)


def fold(value, op):
    rows, width = value.shape
    return op(value.reshape(rows // 8, 8, width), axis=0)


def joined(op, total, value):
    return value if total is None else op(total, value)


class Shape:
    def __init__(self, blocks, width, heads, group):
        self.blocks, self.width, self.heads, self.group = blocks, width, heads, group

    def rows(self, row):
        return slice(row * BLK, (row + 1) * BLK)

    def lanes(self, head):
        return slice(head * HD, (head + 1) * HD)

    def parts(self, head):
        first = head * self.group
        return [slice((first + g) * HD, (first + g + 1) * HD) for g in range(self.group)]

    def wide(self, head):
        return slice(head * self.group * HD, (head + 1) * self.group * HD)

    def chunks(self):
        return [(c, slice(c * BLK, (c + 1) * BLK)) for c in range(self.width)]

    def entry(self, row, column):
        return row * self.width + column

    def stacked(self, ref, row, head):
        return jnp.concatenate([ref[self.rows(row), part] for part in self.parts(head)], axis=0)

    def flipped(self, ref, row, head):
        return jnp.concatenate([ref[self.rows(row), part].T for part in self.parts(head)], axis=1)


def first_exps_kernel(pieces, dims, tokens, place_ref, tp_ref, query_hbm, grad_hbm, *refs):
    count = len(pieces)
    exp_ref, grad_t_ref, inv_ref, acc, buffer, query, grad, score_ref, sems = refs[count:]
    copies = []
    for head in range(dims.heads):
        for source, target in ((query_hbm, query), (grad_hbm, grad)):
            lanes = dims.wide(head)
            copies.append(
                pltpu.make_async_copy(source.at[:, lanes], target.at[:, lanes], sems.at[len(copies)])
            )
            copies[-1].start()
    place_pieces(refs[:count], pieces, tokens, tp_ref[0], buffer)
    copies[0].wait()
    copies[1].wait()
    exp_rows(0, dims, place_ref, query, grad, buffer, exp_ref, grad_t_ref, inv_ref, score_ref)
    add_values(acc, dims, place_ref, exp_ref, grad_t_ref)
    for copy in copies[2:]:
        copy.wait()


def exps_kernel(head, dims, tokens, place_ref, tp_ref, query, grad, buffer, *refs):
    accs, refs = refs[:head], refs[head:]
    exp_ref, grad_t_ref, inv_ref, *sum_refs, acc, score_ref = refs
    exp_rows(head, dims, place_ref, query, grad, buffer, exp_ref, grad_t_ref, inv_ref, score_ref)
    add_values(acc, dims, place_ref, exp_ref, grad_t_ref)
    write_sums([*accs, acc], sum_refs, tokens, tp_ref[0], None)


def exp_rows(head, dims, place_ref, query, grad, buffer, exp_ref, grad_t_ref, inv_ref, score_ref):
    factor = LOG2E * float(HD) ** (-0.5)
    lanes = dims.lanes(head)
    tops = {}
    for step in range(dims.blocks + 1):
        first, second = step, step - 1
        top_new = total = None
        if first < dims.blocks:
            stacked = dims.stacked(query, first, head)
        if 0 <= second:
            top = jnp.max(tops[second], axis=0, keepdims=True) * factor
        for column, chunk in dims.chunks():
            if first < dims.blocks:
                keys = buffer[block_of(place_ref, dims.entry(first, column)), lanes]
                score = lax.dot_general(keys, stacked, NT, preferred_element_type=jnp.float32)
                score_ref[first % 2, chunk] = score
                top_new = joined(jnp.maximum, top_new, fold(score, jnp.max))
            if 0 <= second:
                weight = jnp.exp2(score_ref[second % 2, chunk] * factor - top)
                exp_ref[second, chunk] = weight.astype(jnp.bfloat16)
                total = joined(jnp.add, total, fold(weight, jnp.sum))
        tops[first] = top_new
        if 0 <= second:
            inverse = 1.0 / jnp.sum(total, axis=0, keepdims=True)
            inv_ref[second] = jnp.broadcast_to(inverse, inv_ref.shape[1:])
            grad_t = dims.flipped(grad, second, head).astype(jnp.float32)
            grad_t_ref[second] = (grad_t * inverse).astype(jnp.bfloat16)


def add_values(acc, dims, place_ref, exp_ref, grad_t_ref):
    acc[...] = jnp.zeros_like(acc)
    for row in range(dims.blocks):
        for column, chunk in dims.chunks():
            acc[block_of(place_ref, dims.entry(row, column))] += lax.dot_general(
                exp_ref[row, chunk], grad_t_ref[row], NT, preferred_element_type=jnp.float32
            )


def add_keys(acc, dims, place_ref, row, head, ds_ref, query):
    stacked = dims.stacked(query, row, head)
    for column, chunk in dims.chunks():
        acc[block_of(place_ref, dims.entry(row, column)), dims.lanes(head)] += jnp.dot(
            ds_ref[row, chunk], stacked, preferred_element_type=jnp.float32
        )


def score_rows(head, dims, place_ref, exp_ref, grad_t_ref, inv_ref, buffer, out_ref, ds_ref, listed, then):
    lanes = dims.lanes(head)
    for row in range(dims.blocks):
        slot = row % 2
        for column, chunk in dims.chunks():
            listed[slot, chunk] = buffer[block_of(place_ref, dims.entry(row, column)), lanes]
        attended = lax.dot_general(
            listed[slot], exp_ref[row], TN, preferred_element_type=jnp.float32
        )
        attended = (attended * inv_ref[row, 0:1]).astype(jnp.bfloat16)
        grad_t = grad_t_ref[row]
        delta = jnp.sum(
            grad_t.astype(jnp.float32) * attended.astype(jnp.float32), axis=0, keepdims=True
        )
        for g, part in enumerate(dims.parts(0)):
            out_ref[dims.rows(row), part] = attended[:, g * BLK : (g + 1) * BLK].T
        for column, chunk in dims.chunks():
            dprob = jnp.dot(listed[slot, chunk], grad_t, preferred_element_type=jnp.float32)
            weight = exp_ref[row, chunk].astype(jnp.float32)
            ds_ref[row, chunk] = (weight * (dprob - delta)).astype(jnp.bfloat16)
        then(row)


def scores_kernel(head, pieces, dims, tokens, place_ref, tp_ref, exp_ref, grad_t_ref, inv_ref, *refs):
    count = len(pieces)
    out_ref, ds_ref, buffer, flag_ref, listed = refs[count:]
    flag_ref[...] = jnp.zeros_like(flag_ref)
    place_pieces(refs[:count], pieces, tokens, tp_ref[0], buffer)
    score_rows(
        head, dims, place_ref, exp_ref, grad_t_ref, inv_ref, buffer, out_ref, ds_ref, listed,
        lambda row: None,
    )


def keys_kernel(dims, tokens, place_ref, tp_ref, exp_ref, grad_t_ref, inv_ref, buffer, *refs):
    done_refs, query = refs[: dims.heads - 1], refs[dims.heads - 1]
    out_ref, ds_ref, *sum_refs, acc, listed = refs[dims.heads :]
    acc[...] = jnp.zeros_like(acc)

    def then(row):
        for head, done_ref in enumerate(done_refs):
            add_keys(acc, dims, place_ref, row, head, done_ref, query)
        add_keys(acc, dims, place_ref, row, dims.heads - 1, ds_ref, query)

    score_rows(
        dims.heads - 1, dims, place_ref, exp_ref, grad_t_ref, inv_ref, buffer, out_ref, ds_ref,
        listed, then,
    )
    write_sums([acc], sum_refs, tokens, tp_ref[0], float(HD) ** (-0.5))


def rows_kernel(dims, place_ref, buffer_ref, *refs):
    weight_refs = refs[: dims.heads]
    out_ref, flag_ref, listed = refs[dims.heads :]
    flag_ref[...] = jnp.zeros_like(flag_ref)
    for row in range(dims.blocks):
        for head in range(dims.heads):
            for column, chunk in dims.chunks():
                block = block_of(place_ref, dims.entry(row, column))
                listed[head % 2, chunk] = buffer_ref[block, dims.lanes(head)]
            result = lax.dot_general(
                listed[head % 2], weight_refs[head][row], TN, preferred_element_type=jnp.float32
            )
            result = (result * float(HD) ** (-0.5)).astype(jnp.bfloat16)
            for g, part in enumerate(dims.parts(head)):
                out_ref[dims.rows(row), part] = result[:, g * BLK : (g + 1) * BLK].T


def to_head_groups(rows):
    me = lax.axis_index("tp")
    count = lax.axis_size("tp")
    width = rows.shape[1] // count
    parts = {}
    for mask in reversed(range(count)):
        part = lax.dynamic_slice_in_dim(rows, (me ^ mask) * width, width, 1)
        parts[mask] = part if mask == 0 else swap(part, "tp", mask)
    return jnp.stack([parts[mask] for mask in range(count)])


def to_quarters(pieces):
    me = lax.axis_index("tp")
    count, quarter, width = pieces.shape
    out = jnp.zeros((quarter, count * width), pieces.dtype)
    for mask in range(count):
        part = pieces[mask] if mask == 0 else swap(pieces[mask], "tp", mask)
        out = lax.dynamic_update_slice(out, part, (0, (me ^ mask) * width))
    return out


def cut(*values):
    return lax.optimization_barrier(values)


def held_until(value, *others):
    return lax.optimization_barrier((value, *others))[0]


def with_near(own):
    return swap(own, "ctx", 2), swap(own, "ctx", 4)


def swap_diagonal(value):
    count = lax.axis_size("ctx")
    return lax.ppermute(value, "ctx", [(i, i ^ (4 if i % 2 else 2)) for i in range(count)])


def pick(first, second):
    odd = lax.axis_index("ctx") % 2 == 1
    return jnp.where(odd, second, first)


def to_neighbours(near, got, diagonal):
    nothing = jnp.zeros_like(diagonal)
    to_x = near[1] + got[1] + pick(nothing, diagonal)
    to_y = near[2] + got[2] + pick(diagonal, nothing)
    return to_x, to_y


def total_own(near, got, from_x, from_y):
    return near[0] + got[0] + from_x + from_y


def dense_plan(queries, key_rows, value_rows, out_grad, block_list):
    tokens = queries.shape[0]
    blocks = tokens // BLK
    shard_total = lax.axis_size("ctx")
    quarters = lax.axis_size("tp")
    width = block_list.shape[1]
    head_width = key_rows.shape[1] // quarters
    heads = head_width // HD
    group = queries.shape[1] // head_width
    rows = shard_total * tokens
    me_ctx = lax.axis_index("ctx")
    me_tp = lax.axis_index("tp").reshape(1)
    places = ((block_list // blocks) ^ me_ctx) * blocks + block_list % blocks
    places = places.reshape(-1)
    quarter = tokens // quarters
    pieces = [((shard,), 0, quarters) for shard in (0, 2, 4, 6)]
    pieces += [((1, 3, 5), 0, quarters), ((7,), 0, quarters)]
    dims = Shape(blocks, width, heads, group)
    list_len = width * BLK
    query_rows = group * BLK
    bf16 = jnp.bfloat16

    in_vmem = pl.BlockSpec(memory_space=pltpu.VMEM)
    in_smem = pl.BlockSpec(memory_space=pltpu.SMEM)
    in_hbm = pl.BlockSpec(memory_space=pltpu.HBM)
    queries = pltpu.with_memory_space_constraint(queries, pltpu.HBM)
    out_grad = pltpu.with_memory_space_constraint(out_grad, pltpu.HBM)
    shape = jax.ShapeDtypeStruct
    sums = [shape((shard_total // 2, quarters, quarter, head_width), bf16)] * 2
    stash = shape((blocks, list_len, query_rows), bf16)
    grads = shape((blocks, HD, query_rows), bf16)
    inverses = shape((blocks, 8, query_rows), jnp.float32)
    ordered = shape((rows, head_width), bf16)
    flat = shape(queries.shape, bf16)
    flag = shape((8, HD), jnp.float32)
    one_head = shape((tokens, group * HD), bf16)
    two_rows = pltpu.VMEM((2, list_len, query_rows), jnp.float32)
    total = pltpu.VMEM((rows, head_width), jnp.float32)
    head_sum = shape((rows, HD), jnp.float32)
    head_total = pltpu.VMEM((rows, HD), jnp.float32)
    listed = pltpu.VMEM((2, list_len, HD), bf16)
    sem = pltpu.SemaphoreType.DMA

    def call(name, kernel, outs, scratch, scalars, operands):
        return pl.pallas_call(
            kernel,
            in_specs=[in_smem] * len(scalars) + [in_hbm if x is queries or x is out_grad else in_vmem for x in operands],
            out_specs=[in_vmem] * len(outs),
            out_shape=outs,
            scratch_shapes=scratch,
            compiler_params=pltpu.CompilerParams(vmem_limit_bytes=VMEM_MIB * 2**20),
            cost_estimate=pl.CostEstimate(flops=2**32, bytes_accessed=2**20, transcendentals=0),
            name=name,
        )(*scalars, *operands)

    key_own = to_head_groups(key_rows)
    key_x, key_y = with_near(key_own)
    value_own = to_head_groups(value_rows)
    key_x, key_y, key_own, value_own = cut(key_x, key_y, key_own, value_own)
    key_next, key_x, key_y, key_own = cut(pick(key_y, key_x), key_x, key_y, key_own)
    key_three = jnp.concatenate([key_own, key_x, key_y])
    key_diag, key_three = cut(swap_diagonal(key_next), key_three)
    keys = [key_own, key_x, key_y, key_diag]
    keys += [swap(part, "ctx", 1) for part in (key_three, key_diag)]
    value_x, value_y = with_near(held_until(value_own, key_diag))

    exp_0, grad_0, inverse_0, sum_0, keys_in_order, query_here, grad_here = call(
        "exps_0", functools.partial(first_exps_kernel, pieces, dims, tokens),
        [stash, grads, inverses, head_sum, ordered, flat, flat], [two_rows, sem((2 * heads,))],
        (places, me_tp), (queries, out_grad, *keys),
    )
    value_x, value_y, inverse_0 = cut(value_x, value_y, inverse_0)
    value_next, value_three, places_1 = cut(
        pick(value_y, value_x), jnp.concatenate([value_own, value_x, value_y]), places
    )
    value_diag = swap_diagonal(value_next)
    value_far = swap(value_three, "ctx", 1)
    exp_1, grad_1, inverse_1, value_near, value_away = call(
        "exps", functools.partial(exps_kernel, 1, dims, tokens),
        [stash, grads, inverses, *sums], [head_total, two_rows], (places_1, me_tp),
        (query_here, grad_here, keys_in_order, sum_0),
    )
    exps, grad_ts, inverse = (exp_0, exp_1), (grad_0, grad_1), (inverse_0, inverse_1)
    value_diag, value_far, value_near, value_away = cut(
        value_diag, value_far, value_near, value_away
    )
    value_last = swap(value_diag, "ctx", 1)
    value_away, places_2, value_last = cut(value_away, places, value_last)
    values = [value_own, value_x, value_y, value_diag, value_far, value_last]
    value_got = swap(value_away, "ctx", 1)
    ds, token, attended = [], None, []
    for head in range(heads - 1):
        out, made, values_in_order, token = call(
            "scores", functools.partial(scores_kernel, head, pieces, dims, tokens),
            [one_head, stash, ordered, flag], [listed], (places_2, me_tp),
            (exps[head], grad_ts[head], inverse[head], *values),
        )
        attended.append(out)
        ds.append(made)
    value_got, token = cut(value_got, token)
    diagonal, places_3 = cut(value_near[3] + value_got[3], held_until(places, token))
    value_first = swap_diagonal(diagonal)
    out, made, key_near, key_away = call(
        "key_sums", functools.partial(keys_kernel, dims, tokens),
        [one_head, stash, *sums], [total, listed], (places_3, me_tp),
        (exps[-1], grad_ts[-1], inverse[-1], values_in_order, *ds, query_here),
    )
    attended.append(out)
    ds.append(made)
    key_near, key_away, places_4, value_first = cut(key_near, key_away, places, value_first)
    key_got = swap(key_away, "ctx", 1)
    to_x, to_y = to_neighbours(value_near, value_got, value_first)
    value_more = swap(to_x, "ctx", 2), swap(to_y, "ctx", 4)
    query_grad, token = call(
        "query_grad", functools.partial(rows_kernel, dims),
        [flat, flag], [listed], (places_4,), (keys_in_order, *ds),
    )
    key_got, token = cut(key_got, token)
    diagonal = held_until(key_near[3] + key_got[3], token)
    key_first = swap_diagonal(diagonal)
    attended = jnp.concatenate(cut(*attended, diagonal)[:heads], axis=1)
    attended, *value_more = cut(attended, *value_more)
    value_sum = total_own(value_near, value_got, *value_more)
    key_first, attended = cut(key_first, attended)
    to_x, to_y = to_neighbours(key_near, key_got, key_first)
    value_grad = to_quarters(value_sum)
    key_more = swap(to_x, "ctx", 2), swap(to_y, "ctx", 4)
    key_sum = total_own(key_near, key_got, *key_more)
    return attended, query_grad, to_quarters(key_sum), value_grad


def solution(mesh):
    dense = mesh.shape["ctx"] == DENSE_SHARDS and mesh.shape["tp"] % 4 == 0
    in_specs = (
        P("ctx", "tp"),
        P(("ctx", "tp"), None),
        P(("ctx", "tp"), None),
        P("ctx", "tp"),
        P("ctx", None),
    )
    out_specs = (P("ctx", "tp"), P("ctx", "tp"), P(("ctx", "tp"), None), P(("ctx", "tp"), None))
    return jax.shard_map(
        dense_plan if dense else sparse_plan,
        mesh=mesh,
        in_specs=in_specs,
        out_specs=out_specs,
        check_vma=False,
    )
```
